128 devices in a mesh: group: 8 (over z, core), dev: 16 (over y, x).
Axes of the slice: x: 4, y: 4, z: 4, core: 2. Of those that a mesh axis runs over, the one named last changes fastest.
Arguments:
- parent_front: float32 [8192, 8192], P('group', 'dev'), may hold values from -16 to 60, as said below
- child_front: bfloat16 [8, 4096, 1536], P('group', 'dev'), may hold values from -0.020817695 to 0.020817695
- inverse_factor: bfloat16 [8, 1536, 1536], P('group', 'dev'), may hold values from -0.102062073 to 0.102062073
- child_index: int32 [8, 32], replicated, may hold values from 0 to 63, as said below
- child_blocks: int32 [8], replicated, may hold values from 1 to 32, 192 in all
Outputs:
- front: float32 [8192, 8192], P('group', 'dev')
The draws below stay inside these ranges and needn't reach their ends.
Inputs may be any that keep to these rules, and one draw needn't show every extreme that they name: `child_index`: row g lists distinct parent blocks in rising order, exactly 4 of them in each of the 8 row slots of 8 consecutive blocks; only its first child_blocks[g] entries are live. `parent_front`: Symmetric; no entry off the diagonal is positive; each diagonal entry exceeds the sum of the magnitudes of the other entries of its row.
All inputs are finite; a program needn't handle non-finite values.
Results may differ from the reference program's by a relative error of at most 0.00065.
Values may be sent and summed in bfloat16 or wider, within the bound.
A program may use at most 128 MiB of HBM per device.

```python
import math
import jax
import jax.numpy as jnp
import numpy as np
from jax import lax

N = 8192
U = 4096
PIV = 1536
BLK = 128
PANELS = 4
N_GROUP = 8


def log_uniform(one_key, count, lower, upper):
    spread = jax.random.uniform(one_key, (count,), jnp.float32, jnp.log(lower), jnp.log(upper))
    return jnp.clip(jnp.exp(spread), lower, upper)


def draw_parent_front(key, part):
    key = jax.random.fold_in(key, 7)
    subkeys = jax.random.split(key, 5)
    pivots = PANELS * BLK
    trailing = N - pivots
    ranking = jax.random.permutation(subkeys[0], trailing).astype(jnp.int32)
    leaves = jnp.where(ranking < 3 * pivots, ranking % pivots, -1).astype(jnp.int32)
    partner = jnp.concatenate([jnp.full((pivots,), -1, jnp.int32), leaves])
    cycle = jax.random.permutation(subkeys[1], pivots).astype(jnp.int32)
    follow = jnp.concatenate([cycle, jnp.full((trailing,), -1, jnp.int32)])
    leaf_weight = log_uniform(subkeys[2], N, 1.0, 8.0)
    link_weight = log_uniform(subkeys[3], N, 4.0, 16.0)
    margin = log_uniform(subkeys[4], N, 1.2, 2.4)
    indices = jnp.arange(N, dtype=jnp.int32)
    to_pivot = partner[None, :] == indices[:, None]
    from_leaf = partner[:, None] == indices[None, :]
    same = indices[:, None] == indices[None, :]
    chained = ((follow[:, None] == indices[None, :]) | (follow[None, :] == indices[:, None])) & jnp.logical_not(same)
    coupling = jnp.sqrt(link_weight[:, None] * link_weight[None, :])
    outside = jnp.where(to_pivot, -leaf_weight[None, :], jnp.where(from_leaf, -leaf_weight[:, None], jnp.where(chained, -coupling, 0.0)))
    diagonal = margin - jnp.sum(outside, axis=1)
    return jnp.where(same, diagonal[:, None], outside)


def draw_child_front(key, part):
    key = jax.random.fold_in(key, 11)
    scale = 0.9 / (U ** 0.5 + (N_GROUP * PIV) ** 0.5)
    values = jnp.clip(jax.random.normal(key, (N_GROUP, U, PIV), jnp.float32), -4.0, 4.0)
    return (values * scale).astype(jnp.bfloat16)


def draw_inverse_factor(key, part):
    key = jax.random.fold_in(key, 13)
    scale = 1.0 / PIV ** 0.5
    values = jnp.clip(jax.random.normal(key, (N_GROUP, PIV, PIV), jnp.float32), -4.0, 4.0)
    return (values * scale).astype(jnp.bfloat16)


def pick_slot(one_key):
    slot_blocks = N // (BLK * N_GROUP)
    per_slot = U // (BLK * N_GROUP)
    return jax.random.permutation(one_key, slot_blocks)[:per_slot]


def draw_child_index(key, part):
    key = jax.random.fold_in(key, 5)
    slot_blocks = N // (BLK * N_GROUP)
    per_slot = U // (BLK * N_GROUP)
    subkeys = jax.random.split(key, N_GROUP * N_GROUP)
    chosen = jnp.sort(jax.vmap(pick_slot)(subkeys), axis=1)
    chosen = chosen.at[0, 0].set(0)
    chosen = chosen.at[N_GROUP - 1, per_slot - 1].set(slot_blocks - 1)
    offsets = jnp.arange(N_GROUP * N_GROUP) % N_GROUP * slot_blocks
    return (chosen + offsets[:, None]).reshape(N_GROUP, N_GROUP * per_slot).astype(jnp.int32)


def profile(number_of, total, reach, slope):
    weights = [(1 << 20) // math.isqrt(grade ** slope) + 1 for grade in range(2, number_of + 1)]
    spare, holding = total - reach - (number_of - 1), [1] * (number_of - 1)
    while spare > 0:
        candidates = [i for i in range(number_of - 1) if holding[i] < reach]
        whole, remaining = sum([weights[i] for i in candidates]), spare
        for i in candidates:
            extra = min(reach - holding[i], max(1, remaining * weights[i] // whole), spare)
            holding[i] = holding[i] + extra
            spare = spare - extra
    return np.array([reach] + holding)


def uneven_parts(stream_key, number_of, total, reach, lean):
    if number_of == 2:
        one = jax.random.randint(stream_key, (), max(1, total - reach), min(reach, total - 1) + 1)
        return jnp.stack([one, total - one])
    sizes = jnp.asarray(profile(number_of, total, reach, lean), jnp.int32)
    pairs = (number_of - 1) // 2
    donor, receiver = sizes[1:1 + 2 * pairs:2], sizes[2:2 + 2 * pairs:2]
    room = jnp.minimum(donor - 1, reach - receiver)
    moved = jax.random.randint(jax.random.fold_in(stream_key, 1), (pairs,), 0, 1 << 20) % (room + 1)
    sizes = sizes.at[1:1 + 2 * pairs:2].set(donor - moved).at[2:2 + 2 * pairs:2].set(receiver + moved)
    return sizes[jax.random.permutation(jax.random.fold_in(stream_key, 2), number_of)]


def setup_inputs(seed: int = 0) -> dict:
    splits = jax.random.split(jax.random.key(seed), 6)
    parent_front = draw_parent_front(jax.random.fold_in(splits[5], 71), 0)
    child_front = draw_child_front(jax.random.fold_in(splits[5], 71), 0)
    inverse_factor = draw_inverse_factor(jax.random.fold_in(splits[5], 71), 0)
    child_index = draw_child_index(jax.random.fold_in(splits[5], 71), 0)
    child_blocks = uneven_parts(splits[4], N_GROUP, N_GROUP * (U // BLK) * 3 // 4, U // BLK, 2).astype(jnp.int32)
    return dict(parent_front=parent_front, child_front=child_front, inverse_factor=inverse_factor, child_index=child_index, child_blocks=child_blocks)


def reference(parent_front, child_front, inverse_factor, child_index, child_blocks):
    blocks = U // BLK
    slots = N // BLK
    front = parent_front.reshape(slots, BLK, slots, BLK)
    for child in range(N_GROUP):
        product = jnp.dot(child_front[child].astype(jnp.float32), inverse_factor[child].astype(jnp.float32), preferred_element_type=jnp.float32)
        live = (jnp.arange(U) // BLK < child_blocks[child]).astype(jnp.float32)
        factor = (product * live[:, None]).astype(jnp.bfloat16)
        factor = lax.optimization_barrier(factor).astype(jnp.float32)
        update = -jnp.dot(factor, factor.T, precision=lax.Precision.HIGHEST)
        update = update.reshape(blocks, BLK, blocks, BLK).transpose(0, 2, 1, 3)
        where_to = child_index[child]
        front = front.at[where_to[:, None], :, where_to[None, :], :].add(update)
    front = front.reshape(N, N)
    for step in range(PANELS):
        low = step * BLK
        high = low + BLK
        pivot = jnp.linalg.cholesky(front[low:high, low:high])
        below = jax.scipy.linalg.solve_triangular(pivot, front[high:, low:high].T, lower=True).T
        trail = front[high:, high:] - jnp.dot(below, below.T, precision=lax.Precision.HIGHEST)
        front = front.at[high:, high:].set(trail)
        front = front.at[low:high, low:high].set(pivot)
        front = front.at[high:, low:high].set(below)
        front = front.at[low:high, high:].set(jnp.zeros((BLK, N - high), jnp.float32))
    return front
```

```python
import jax
import jax.numpy as jnp
from jax import lax
from jax.experimental import pallas as pl
from jax.experimental.pallas import tpu as pltpu
from jax.sharding import PartitionSpec as P

N = 8192
BLK = 128
PANELS = 4
PIV_COLS = BLK * PANELS
MESH = pl.DeviceIdType.MESH
EXACT = lax.Precision.HIGHEST
STRIP = 16


def dot(a, b, contract, precision=EXACT):
    return lax.dot_general(
        a, b, (contract, ((), ())), precision=precision, preferred_element_type=jnp.float32
    )


class Place:
    def __init__(self):
        self.group = lax.axis_index("group")
        self.dev = lax.axis_index("dev")
        self.x = self.dev % 4
        self.y = self.dev // 4
        self.z = self.group // 2
        self.core = self.group % 2
        self.right = (self.group, self.y * 4 + (self.x + 1) % 4)
        self.left = (self.group, self.y * 4 + (self.x + 3) % 4)
        self.down = (self.group, (self.y + 1) % 4 * 4 + self.x)
        self.up = (self.group, (self.y + 3) % 4 * 4 + self.x)
        self.above = ((self.z + 1) % 4 * 2 + self.core, self.dev)
        self.below = ((self.z + 3) % 4 * 2 + self.core, self.dev)
        self.mate = (self.z * 2 + 1 - self.core, self.dev)

    def rows_first(self):
        x, y = self.x, self.y
        return [
            ((y == 0) & (x < 2), self.right),
            (((y == 0) & (x == 0)) | ((x == 1) & (y != 0)), self.left),
            ((x != 0) & (y < 2), self.down),
            ((x != 0) & (y == 0), self.up),
        ]

    def cols_first(self):
        x, y = self.x, self.y
        return [
            ((x == 0) & (y < 2), self.down),
            (((x == 0) & (y == 0)) | ((y == 1) & (x != 0)), self.up),
            ((y != 0) & (x < 2), self.right),
            ((y != 0) & (x == 0), self.left),
        ]

    def through_groups(self):
        z, core = self.z, self.core
        return [
            ((core == 0) & (z < 2), self.above),
            ((core == 0) & (z == 0), self.below),
            (core == 0, self.mate),
        ]

    def everywhere(self):
        edges = [(cond & (self.group == 0), to) for cond, to in self.rows_first()]
        return edges + self.through_groups()


def remote(src, dst, send, recv, to):
    return pltpu.make_async_remote_copy(
        src_ref=src, dst_ref=dst, send_sem=send, recv_sem=recv, device_id=to, device_id_type=MESH
    )


def forward(edges, ref, sends, recv):
    for e, (cond, to) in enumerate(edges):
        @pl.when(cond)
        def _(e=e, to=to):
            remote(ref, ref, sends.at[e], recv, to).start()


def wait_sends(edges, ref, sends, recv):
    for e, (cond, to) in enumerate(edges):
        @pl.when(cond)
        def _(e=e, to=to):
            remote(ref, ref, sends.at[e], recv, to).wait_send()


def factor_block(work):
    for s in range(BLK // STRIP):
        top = s * STRIP
        strip = work[top : top + STRIP, :]
        cols = [
            jnp.broadcast_to(strip[:, top + i : top + i + 1], (STRIP, BLK)) for i in range(STRIP)
        ]
        row_id = lax.broadcasted_iota(jnp.int32, (STRIP, BLK), 0)
        for i in range(STRIP):
            root = lax.rsqrt(cols[i][i : i + 1, :])
            scaled = strip[i : i + 1, :] * jnp.concatenate([root, root], axis=1)
            under = jnp.where(row_id > i, cols[i] * root, 0.0)
            under2 = jnp.concatenate([under, under], axis=1)
            at = jnp.concatenate([row_id, row_id], axis=1) == i
            strip = jnp.where(at, scaled, strip - under2 * scaled)
            for k in range(i + 1, STRIP):
                cols[k] = cols[k] - under * (cols[k][i : i + 1, :] * root)
        work[top : top + STRIP, :] = strip
        rest = top + STRIP
        if rest < BLK:
            work[rest:, :] = work[rest:, :] - dot(strip[:, rest:BLK], strip, ((0,), (0,)))


def eliminate(here, tile, out, panel, across, msg, corner, work, sems):
    panel_send, panel_recv, across_send, across_recv, msg_send, msg_recv = sems
    group, dev = here.group, here.dev
    rows = tile.shape[0]
    half = rows // 2
    first = (group == 0) & (dev == 0)
    step = half // 4

    def panel_ref(h, c):
        return panel.at[pl.ds(h * half + c * step, step), :]

    def across_ref(c):
        return across.at[pl.ds(c * BLK, BLK), :]

    trees = (here.rows_first(), here.cols_first())
    zedges = here.through_groups()
    every = here.everywhere()

    @pl.when(dev == 0)
    def _():
        panel[...] = tile[...]

    @pl.when(group == 0)
    def _():
        across[...] = tile[0:PIV_COLS, :]

    @pl.when(first)
    def _():
        corner[...] = tile[0:PIV_COLS, :]

    for c in range(4):
        for h in range(2):
            sem = panel_recv.at[h * 4 + c]
            ref = panel_ref(h, c)

            @pl.when(dev != 0)
            def _():
                remote(ref, ref, sem, sem, here.left).wait_recv()

            forward(trees[h], ref, panel_send.at[h * 4 + c], sem)

        @pl.when(group != 0)
        def _():
            ref = across_ref(c)
            remote(ref, ref, across_recv.at[c], across_recv.at[c], here.above).wait_recv()

        forward(zedges, across_ref(c), across_send.at[c], across_recv.at[c])

    def settle():
        for c in range(4):
            for h in range(2):
                wait_sends(trees[h], panel_ref(h, c), panel_send.at[h * 4 + c], panel_recv.at[h * 4 + c])
            wait_sends(zedges, across_ref(c), across_send.at[c], across_recv.at[c])

    @pl.when(jnp.logical_not(first))
    def _():
        settle()

        @pl.when(dev != 0)
        def _():
            out[...] = tile[...]

    def msg_ref(k):
        return msg.at[k, :, k * BLK : PIV_COLS]

    def consume(k):
        low = k * BLK
        inverse = msg[k, :, low : low + BLK]
        q_across = dot(inverse, across[low : low + BLK, :], ((1,), (0,)))
        for piece in range(4):
            at = pl.ds(piece * (rows // 4), rows // 4)
            q_rows = dot(panel[at, low : low + BLK], inverse, ((1,), (1,)))
            if k < PANELS - 1:
                high = low + BLK
                panel[at, high:PIV_COLS] = panel[at, high:PIV_COLS] - dot(
                    q_rows, msg[k, :, high:PIV_COLS], ((1,), (0,))
                )

            @pl.when(dev == 0)
            def _():
                out[at, low : low + BLK] = q_rows

            @pl.when(dev != 0)
            def _():
                out[at, :] = out[at, :] - dot(q_rows, q_across, ((1,), (0,)))

        if k < PANELS - 1:
            high = low + BLK
            across[high:PIV_COLS, :] = across[high:PIV_COLS, :] - dot(
                msg[k, :, high:PIV_COLS], q_across, ((0,), (0,))
            )

    diag = lax.broadcasted_iota(jnp.int32, (BLK, BLK), 0) - lax.broadcasted_iota(jnp.int32, (BLK, BLK), 1)

    def one_panel(k, _):
        @pl.when(first)
        def _():
            for kk in range(PANELS):
                @pl.when(k == kk)
                def _():
                    work[:, 0:BLK] = corner[kk * BLK : (kk + 1) * BLK, kk * BLK : (kk + 1) * BLK]

            work[:, BLK:] = jnp.where(diag == 0, 1.0, 0.0)
            factor_block(work)
            inverse = jnp.where(diag >= 0, work[:, BLK:], 0.0)
            for kk in range(PANELS):
                @pl.when(k == kk)
                def _():
                    low, high = kk * BLK, (kk + 1) * BLK
                    msg[kk, :, low:high] = inverse
                    if kk < PANELS - 1:
                        strip = dot(inverse, corner[low:high, high:], ((1,), (0,)))
                        msg[kk, :, high:] = strip
                        corner[high:, high:] = corner[high:, high:] - dot(strip, strip, ((0,), (0,)))
                    corner[low:high, low:high] = jnp.where(diag <= 0, work[:, 0:BLK], 0.0)

        for kk in range(PANELS):
            @pl.when(k == kk)
            def _():
                ref = msg_ref(kk)

                @pl.when(jnp.logical_not(first))
                def _():
                    remote(ref, ref, msg_recv.at[kk], msg_recv.at[kk], here.left).wait_recv()

                forward(every, ref, msg_send.at[kk], msg_recv.at[kk])

                @pl.when(jnp.logical_not(first))
                def _():
                    consume(kk)

        return 0

    lax.fori_loop(0, PANELS, one_panel, 0)

    @pl.when(first)
    def _():
        settle()
        for k in range(PANELS):
            consume(k)
        out[0:PIV_COLS, :] = jnp.zeros((PIV_COLS, PIV_COLS), jnp.float32)
        for k in range(PANELS):
            low, high = k * BLK, (k + 1) * BLK
            out[low:high, low:high] = corner[low:high, low:high].T
            for i in range(k + 1, PANELS):
                out[i * BLK : (i + 1) * BLK, low:high] = msg[k, :, i * BLK : (i + 1) * BLK].T

    @pl.when((group == 0) & (dev != 0))
    def _():
        out[0:PIV_COLS, :] = jnp.zeros((PIV_COLS, PIV_COLS), jnp.float32)

    for k in range(PANELS):
        wait_sends(every, msg_ref(k), msg_send.at[k], msg_recv.at[k])


def greet(targets, count):
    barrier = pltpu.get_barrier_semaphore()
    for to in targets:
        pl.semaphore_signal(barrier, inc=1, device_id=to, device_id_type=MESH)
    pl.semaphore_wait(barrier, count)


def neighbours(here):
    return [here.right, here.left, here.down, here.up, here.above, here.below, here.mate]


def panel_kernel(tile, out, panel, across, msg, corner, work, *sems):
    here = Place()
    greet(neighbours(here), 7)
    eliminate(here, tile, out, panel, across, msg, corner, work, sems)


DMA = pltpu.SemaphoreType.DMA


def panel_scratch(rows, cols):
    return [
        pltpu.VMEM((rows, PIV_COLS), jnp.float32),
        pltpu.VMEM((PIV_COLS, cols), jnp.float32),
        pltpu.VMEM((PANELS, BLK, PIV_COLS), jnp.float32),
        pltpu.VMEM((PIV_COLS, PIV_COLS), jnp.float32),
        pltpu.VMEM((BLK, 2 * BLK), jnp.float32),
        DMA((8, 4)),
        DMA((8,)),
        DMA((4, 3)),
        DMA((4,)),
        DMA((PANELS, 7)),
        DMA((PANELS,)),
    ]


def eliminate_panels(assembled):
    rows, cols = assembled.shape
    return pl.pallas_call(
        panel_kernel,
        out_shape=jax.ShapeDtypeStruct((rows, cols), jnp.float32),
        in_specs=[pl.BlockSpec(memory_space=pltpu.VMEM)],
        out_specs=pl.BlockSpec(memory_space=pltpu.VMEM),
        scratch_shapes=panel_scratch(rows, cols),
        compiler_params=pltpu.CompilerParams(
            collective_id=1, has_side_effects=True, vmem_limit_bytes=40 * 1024 * 1024
        ),
        name="eliminate_panels",
    )(assembled)


def on_device(parent_front, child_front, inverse_factor, child_index, child_blocks):
    rows_here, cols_here = parent_front.shape
    group = lax.axis_index("group")
    device = lax.axis_index("dev")
    groups, blocks = child_index.shape
    own_index = lax.dynamic_index_in_dim(child_index, group, 0, keepdims=False)
    own_count = lax.dynamic_index_in_dim(child_blocks, group, 0, keepdims=False)
    local_front = child_front[0]
    local_rows = local_front.shape[0]
    pivots = inverse_factor.shape[2]
    product = jnp.dot(
        local_front,
        lax.all_gather(inverse_factor, "dev", axis=1, tiled=True)[0],
        preferred_element_type=jnp.float32,
    )
    row_ids = device * local_rows + jnp.arange(local_rows)
    factor = jnp.where((row_ids // BLK < own_count)[:, None], product, 0.0).astype(jnp.bfloat16)
    factor_all = lax.all_gather(factor, "dev", axis=0, tiled=True)
    parent_blocks = N // BLK
    used = jnp.arange(blocks)[None, :] < own_count
    match = (own_index[None, :] == jnp.arange(parent_blocks)[:, None]) & used
    source = jnp.sum(jnp.where(match, jnp.arange(blocks)[None, :], 0), axis=1)
    present = jnp.any(match, axis=1)
    factor_blocks = factor_all.reshape(blocks, BLK, pivots)

    def spread(first, count_blocks):
        pick = lax.dynamic_slice_in_dim(source, first, count_blocks)
        keep = lax.dynamic_slice_in_dim(present, first, count_blocks)
        chosen = jnp.take(factor_blocks, pick, axis=0)
        chosen = jnp.where(keep[:, None, None], chosen, jnp.zeros((), jnp.bfloat16))
        return chosen.reshape(count_blocks * BLK, pivots)

    column_part = spread(device * (cols_here // BLK), cols_here // BLK)
    inner = (((1,), (1,)), ((), ()))
    count = rows_here * lax.axis_size("group")

    def one_block(offset):
        part = spread(offset // BLK, rows_here // BLK)
        return -lax.dot_general(part, column_part, inner, preferred_element_type=jnp.float32)

    pieces = lax.map(one_block, jnp.arange(count // rows_here, dtype=jnp.int32) * rows_here)
    summed = lax.psum_scatter(
        pieces.reshape(count, cols_here).astype(jnp.bfloat16),
        "group",
        scatter_dimension=0,
        tiled=True,
    ).astype(jnp.float32)
    assembled = parent_front + summed
    return eliminate_panels(assembled)


def solution(mesh):
    placed = (P("group", "dev"), P("group", "dev", None), P("group", "dev", None), P(), P())
    return jax.shard_map(
        on_device, mesh=mesh, in_specs=placed, out_specs=P("group", "dev"), check_vma=False
    )
```

```python
import jax
import jax.numpy as jnp
from jax import lax
from jax.experimental import pallas as pl
from jax.experimental.pallas import tpu as pltpu
from jax.sharding import PartitionSpec as P

N = 8192
BLK = 128
PANELS = 4
PIV_COLS = BLK * PANELS
MESH = pl.DeviceIdType.MESH
EXACT = lax.Precision.HIGHEST
STRIP = 16


def dot(a, b, contract, precision=EXACT):
    return lax.dot_general(
        a, b, (contract, ((), ())), precision=precision, preferred_element_type=jnp.float32
    )


class Place:
    def __init__(self):
        self.group = lax.axis_index("group")
        self.dev = lax.axis_index("dev")
        self.x = self.dev % 4
        self.y = self.dev // 4
        self.z = self.group // 2
        self.core = self.group % 2
        self.right = (self.group, self.y * 4 + (self.x + 1) % 4)
        self.left = (self.group, self.y * 4 + (self.x + 3) % 4)
        self.down = (self.group, (self.y + 1) % 4 * 4 + self.x)
        self.up = (self.group, (self.y + 3) % 4 * 4 + self.x)
        self.above = ((self.z + 1) % 4 * 2 + self.core, self.dev)
        self.below = ((self.z + 3) % 4 * 2 + self.core, self.dev)
        self.mate = (self.z * 2 + 1 - self.core, self.dev)

    def rows_first(self):
        x, y = self.x, self.y
        return [
            ((y == 0) & (x < 2), self.right),
            (((y == 0) & (x == 0)) | ((x == 1) & (y != 0)), self.left),
            ((x != 0) & (y < 2), self.down),
            ((x != 0) & (y == 0), self.up),
        ]

    def cols_first(self):
        x, y = self.x, self.y
        return [
            ((x == 0) & (y < 2), self.down),
            (((x == 0) & (y == 0)) | ((y == 1) & (x != 0)), self.up),
            ((y != 0) & (x < 2), self.right),
            ((y != 0) & (x == 0), self.left),
        ]

    def through_groups(self):
        z, core = self.z, self.core
        return [
            ((core == 0) & (z < 2), self.above),
            ((core == 0) & (z == 0), self.below),
            (core == 0, self.mate),
        ]

    def everywhere(self):
        edges = [(cond & (self.group == 0), to) for cond, to in self.rows_first()]
        return edges + self.through_groups()


def remote(src, dst, send, recv, to):
    return pltpu.make_async_remote_copy(
        src_ref=src, dst_ref=dst, send_sem=send, recv_sem=recv, device_id=to, device_id_type=MESH
    )


def forward(edges, ref, sends, recv):
    for e, (cond, to) in enumerate(edges):
        @pl.when(cond)
        def _(e=e, to=to):
            remote(ref, ref, sends.at[e], recv, to).start()


def wait_sends(edges, ref, sends, recv):
    for e, (cond, to) in enumerate(edges):
        @pl.when(cond)
        def _(e=e, to=to):
            remote(ref, ref, sends.at[e], recv, to).wait_send()


def factor_block(work):
    for s in range(BLK // STRIP):
        top = s * STRIP
        strip = work[top : top + STRIP, :]
        cols = [
            jnp.broadcast_to(strip[:, top + i : top + i + 1], (STRIP, BLK)) for i in range(STRIP)
        ]
        row_id = lax.broadcasted_iota(jnp.int32, (STRIP, BLK), 0)
        for i in range(STRIP):
            root = lax.rsqrt(cols[i][i : i + 1, :])
            scaled = strip[i : i + 1, :] * jnp.concatenate([root, root], axis=1)
            under = jnp.where(row_id > i, cols[i] * root, 0.0)
            under2 = jnp.concatenate([under, under], axis=1)
            at = jnp.concatenate([row_id, row_id], axis=1) == i
            strip = jnp.where(at, scaled, strip - under2 * scaled)
            for k in range(i + 1, STRIP):
                cols[k] = cols[k] - under * (cols[k][i : i + 1, :] * root)
        work[top : top + STRIP, :] = strip
        rest = top + STRIP
        if rest < BLK:
            work[rest:, :] = work[rest:, :] - dot(strip[:, rest:BLK], strip, ((0,), (0,)))


def order(here):
    x, y, z = here.x, here.y, here.z

    def hops(k):
        return jnp.minimum(k, 4 - k)

    rows = jnp.where((x == 0) & (y != 0), 2 + hops(y), hops(x) + hops(y))
    cols = jnp.where((y == 0) & (x != 0), 2 + hops(x), hops(x) + hops(y))
    return rows, cols, hops(z) + here.core


CHUNKS = 8


def spread_panel(here, panel, sems):
    send, recv = sems
    half = panel.shape[0] // 2
    step = half // CHUNKS
    trees = (here.rows_first(), here.cols_first())
    depths = order(here)[:2]

    def ref(h, c):
        return panel.at[pl.ds(pl.multiple_of(h * half + c * step, step), step), :]

    def tick(t, _):
        for h in range(2):
            c = t - depths[h]

            @pl.when((c >= 0) & (c < CHUNKS))
            def _():
                @pl.when(here.dev != 0)
                def _():
                    remote(ref(h, c), ref(h, c), recv.at[h, c], recv.at[h, c], here.left).wait_recv()

                forward(trees[h], ref(h, c), send.at[h, c], recv.at[h, c])

        return 0

    lax.fori_loop(0, CHUNKS + 4, tick, 0)


def settle_panel(here, panel, sems):
    send, recv = sems
    half = panel.shape[0] // 2
    step = half // CHUNKS
    for h, tree in enumerate((here.rows_first(), here.cols_first())):
        def one(c, _):
            ref = panel.at[pl.ds(pl.multiple_of(h * half + c * step, step), step), :]
            wait_sends(tree, ref, send.at[h, c], recv.at[h, c])
            return 0

        lax.fori_loop(0, CHUNKS, one, 0)


def spread_across(here, across, sems):
    send, recv = sems
    edges = here.through_groups()

    def ref(c):
        return across.at[pl.ds(pl.multiple_of(c * BLK, BLK), BLK), :]

    def one(c, _):
        @pl.when(here.group != 0)
        def _():
            remote(ref(c), ref(c), recv.at[c], recv.at[c], here.above).wait_recv()

        forward(edges, ref(c), send.at[c], recv.at[c])
        return 0

    def settle():
        def done(c, _):
            wait_sends(edges, ref(c), send.at[c], recv.at[c])
            return 0

        lax.fori_loop(0, PANELS, done, 0)

    lax.fori_loop(0, PANELS, one, 0)
    return settle


def eliminate(here, assemble, out, panel, across, msg, corner, work, sems):
    panel_send, panel_recv, across_send, across_recv, msg_send, msg_recv = sems
    group, dev = here.group, here.dev
    rows = out.shape[0]
    first = (group == 0) & (dev == 0)
    every = here.everywhere()
    panel_sems = (panel_send, panel_recv)

    @pl.when(dev != 0)
    def _():
        spread_panel(here, panel, panel_sems)

    assemble()

    @pl.when(group == 0)
    def _():
        across[...] = out[0:PIV_COLS, :]

    @pl.when(dev == 0)
    def _():
        panel[...] = out[...]
        spread_panel(here, panel, panel_sems)

    settle_across = spread_across(here, across, (across_send, across_recv))

    @pl.when(first)
    def _():
        corner[...] = out[0:PIV_COLS, :]

    def settle():
        settle_panel(here, panel, panel_sems)
        settle_across()

    @pl.when(jnp.logical_not(first))
    def _():
        settle()

    def msg_ref(k):
        return msg.at[k, :, k * BLK : PIV_COLS]

    def consume(k):
        low = k * BLK
        inverse = msg[k, :, low : low + BLK]
        q_across = dot(inverse, across[low : low + BLK, :], ((1,), (0,)))
        for piece in range(4):
            at = pl.ds(piece * (rows // 4), rows // 4)
            q_rows = dot(panel[at, low : low + BLK], inverse, ((1,), (1,)))
            if k < PANELS - 1:
                high = low + BLK
                panel[at, high:PIV_COLS] = panel[at, high:PIV_COLS] - dot(
                    q_rows, msg[k, :, high:PIV_COLS], ((1,), (0,))
                )

            @pl.when(dev == 0)
            def _():
                out[at, low : low + BLK] = q_rows

            @pl.when(dev != 0)
            def _():
                out[at, :] = out[at, :] - dot(q_rows, q_across, ((1,), (0,)))

        if k < PANELS - 1:
            high = low + BLK
            across[high:PIV_COLS, :] = across[high:PIV_COLS, :] - dot(
                msg[k, :, high:PIV_COLS], q_across, ((0,), (0,))
            )

    diag = lax.broadcasted_iota(jnp.int32, (BLK, BLK), 0) - lax.broadcasted_iota(jnp.int32, (BLK, BLK), 1)

    def one_panel(k, _):
        @pl.when(first)
        def _():
            for kk in range(PANELS):
                @pl.when(k == kk)
                def _():
                    work[:, 0:BLK] = corner[kk * BLK : (kk + 1) * BLK, kk * BLK : (kk + 1) * BLK]

            work[:, BLK:] = jnp.where(diag == 0, 1.0, 0.0)
            factor_block(work)
            inverse = jnp.where(diag >= 0, work[:, BLK:], 0.0)
            for kk in range(PANELS):
                @pl.when(k == kk)
                def _():
                    low, high = kk * BLK, (kk + 1) * BLK
                    msg[kk, :, low:high] = inverse
                    if kk < PANELS - 1:
                        strip = dot(inverse, corner[low:high, high:], ((1,), (0,)))
                        msg[kk, :, high:] = strip
                        corner[high:, high:] = corner[high:, high:] - dot(strip, strip, ((0,), (0,)))
                    corner[low:high, low:high] = jnp.where(diag <= 0, work[:, 0:BLK], 0.0)

        for kk in range(PANELS):
            @pl.when(k == kk)
            def _():
                ref = msg_ref(kk)

                @pl.when(jnp.logical_not(first))
                def _():
                    remote(ref, ref, msg_recv.at[kk], msg_recv.at[kk], here.left).wait_recv()

                forward(every, ref, msg_send.at[kk], msg_recv.at[kk])

                @pl.when(jnp.logical_not(first))
                def _():
                    consume(kk)

        return 0

    lax.fori_loop(0, PANELS, one_panel, 0)

    @pl.when(first)
    def _():
        settle()
        for k in range(PANELS):
            consume(k)
        out[0:PIV_COLS, :] = jnp.zeros((PIV_COLS, PIV_COLS), jnp.float32)
        for k in range(PANELS):
            low, high = k * BLK, (k + 1) * BLK
            out[low:high, low:high] = corner[low:high, low:high].T
            for i in range(k + 1, PANELS):
                out[i * BLK : (i + 1) * BLK, low:high] = msg[k, :, i * BLK : (i + 1) * BLK].T

    @pl.when((group == 0) & (dev != 0))
    def _():
        out[0:PIV_COLS, :] = jnp.zeros((PIV_COLS, PIV_COLS), jnp.float32)

    for k in range(PANELS):
        wait_sends(every, msg_ref(k), msg_send.at[k], msg_recv.at[k])


class Ring:
    def __init__(self, region, me, after, before, sems):
        self.after, self.before = after, before
        self.send, self.recv = sems
        width = region(me, slice(None)).shape[-1]
        low, high = slice(0, width // 2), slice(width // 2, width)
        self.own = region(me, slice(None))
        self.prev, self.next = region((me + 3) % 4, slice(None)), region((me + 1) % 4, slice(None))
        self.relays = region((me + 3) % 4, low), region((me + 1) % 4, high)
        self.far = region((me + 2) % 4, low), region((me + 2) % 4, high)

    def copy(self, ref, k, to):
        return remote(ref, ref, self.send.at[k], self.recv.at[k], to)

    def start(self):
        self.copy(self.own, 0, self.after).start()
        self.copy(self.own, 1, self.before).start()

    def relay_prev(self):
        self.copy(self.prev, 0, self.after).wait_recv()
        self.copy(self.relays[0], 2, self.after).start()

    def relay_next(self):
        self.copy(self.next, 1, self.before).wait_recv()
        self.copy(self.relays[1], 3, self.before).start()

    def finish(self):
        self.copy(self.far[0], 2, self.after).wait_recv()
        self.copy(self.far[1], 3, self.before).wait_recv()

    def settle(self):
        self.copy(self.own, 0, self.after).wait_send()
        self.copy(self.own, 1, self.before).wait_send()
        self.copy(self.relays[0], 2, self.after).wait_send()
        self.copy(self.relays[1], 3, self.before).wait_send()


def both(one, two):
    for step in ("relay_prev", "relay_next"):
        getattr(one, step)()
        getattr(two, step)()


def gather_inverse(here, inverse, full, sems):
    send, recv = sems
    rows = full.shape[2]
    low, high = slice(0, rows // 2), slice(rows // 2, rows)
    x, y = here.x, here.y
    full[y, x] = inverse[0]

    def ring(region, me, after, before, k):
        return Ring(region, me, after, before, (send.at[k], recv.at[k]))

    one = ring(lambda p, c: full.at[y, p, low, c], x, here.right, here.left, 0)
    two = ring(lambda p, c: full.at[p, x, high, c], y, here.down, here.up, 1)
    three = ring(lambda p, c: full.at[p, :, low, c], y, here.down, here.up, 2)
    four = ring(lambda p, c: full.at[:, p, high, c], x, here.right, here.left, 3)
    one.start()
    two.start()
    both(one, two)
    one.finish()
    three.start()
    two.finish()
    four.start()
    both(three, four)
    three.finish()
    four.finish()
    return [one, two, three, four]


def child_factor(here, live, front, full, along_x, along_y):
    rows = front.shape[1]
    depth = full.shape[3]
    step = 512
    for low in range(0, depth, step):
        total = jnp.zeros((rows, step), jnp.float32)
        for k in range(4):
            share = full[k, :, :, low : low + step].reshape(depth // 4, step)
            total += dot(front[0, :, k * (depth // 4) : (k + 1) * (depth // 4)], share, ((1,), (0,)), None)
        for b in range(rows // BLK):
            part = slice(b * BLK, (b + 1) * BLK)
            scale = live[here.group, here.dev * (rows // BLK) + b]
            factor = (total[part] * scale).astype(jnp.bfloat16)
            along_x[here.x, part, low : low + step] = factor
            along_y[here.y, part, low : low + step] = factor


def products(here, along_x, along_y, product):
    def one(k, _):
        rows = along_y[k]
        for p in range(4):
            value = dot(rows, along_x[p], ((1,), (1,)), None).astype(jnp.bfloat16)
            product[k, 2 * p] = value[:, 0:BLK]
            product[k, 2 * p + 1] = value[:, BLK:]
        return 0

    lax.fori_loop(0, 4, one, 0)


def send_pieces(here, source, product, pieces, landing, send, recv):
    x, y, z, group = here.x, here.y, here.z, here.group
    slot = group * 2 + x % 2

    def one(step, _):
        to_x, to_z = step // 4, step % 4
        for j in range(4):
            at = ((4 * y + to_x) * 4 + j) * 4
            total = jnp.zeros(product.shape[2:], jnp.float32)
            for i in range(4):
                total += product[to_z, to_x // 2 * 4 + i].astype(jnp.float32) * source[group, at + i]
            pieces[to_z, to_x, :, j * BLK : (j + 1) * BLK] = total.astype(jnp.bfloat16)
        target = (to_z * 2 + x // 2, y * 4 + to_x)
        own = (target[0] == group) & (to_x == x)

        @pl.when(own)
        def _():
            landing[slot] = pieces[to_z, to_x]

        @pl.when(jnp.logical_not(own))
        def _():
            remote(
                pieces.at[to_z, to_x], landing.at[slot], send.at[to_z, to_x], recv.at[slot], target
            ).start()

        return 0

    lax.fori_loop(0, 16, one, 0)

    def settle():
        def done(step, _):
            to_x, to_z = step // 4, step % 4

            @pl.when(jnp.logical_not((to_z * 2 + x // 2 == group) & (to_x == x)))
            def _():
                remote(
                    pieces.at[to_z, to_x], landing.at[slot], send.at[to_z, to_x], recv.at[slot], here.mate
                ).wait_send()

            return 0

        lax.fori_loop(0, 16, done, 0)

    return settle


def sources(here):
    return [
        (g * 2 + p, (g, here.y * 4 + here.core * 2 + p), (here.group == g) & (here.x == here.core * 2 + p))
        for g in range(8)
        for p in range(2)
    ]


def add_pieces(here, source, parent, landing, recv, out):
    group = here.group

    for slot, _, own in sources(here):
        @pl.when(jnp.logical_not(own))
        def _():
            ref = landing.at[slot]
            remote(ref, ref, recv.at[slot], recv.at[slot], here.mate).wait_recv()

    step = 32

    def one(k, _):
        q, r = k // 4, k % 4
        at = pl.ds(pl.multiple_of(k * step, step), step)
        total = jnp.zeros((step, out.shape[1]), jnp.float32)
        for g in range(8):
            for i in range(4):
                row = pl.ds(pl.multiple_of(i % 2 * BLK + r * step, step), step)
                piece = landing[g * 2 + i // 2, row, :].astype(jnp.float32)
                total += piece * source[g, (group * 8 + q) * 4 + i]
        out[at, :] = parent[at, :] - total
        return 0

    lax.fori_loop(0, out.shape[0] // step, one, 0)


def greet(here):
    barrier = pltpu.get_barrier_semaphore()
    for to in [here.right, here.left, here.down, here.up, here.above, here.below, here.mate]:
        pl.semaphore_signal(barrier, inc=1, device_id=to, device_id_type=MESH)
    for _, to, own in sources(here):
        @pl.when(jnp.logical_not(own))
        def _():
            pl.semaphore_signal(barrier, inc=1, device_id=to, device_id_type=MESH)
    pl.semaphore_wait(barrier, jnp.where(here.core == here.x // 2, 22, 23))


def front_kernel(
    source, live, parent, front, inverse, out,
    full, along_x, along_y, product, pieces, landing,
    inverse_send, inverse_recv, factor_send, factor_recv, piece_send, piece_recv,
    panel, across, msg, corner, work, *sems
):
    here = Place()
    greet(here)
    rings = gather_inverse(here, inverse, full, (inverse_send, inverse_recv))
    child_factor(here, live, front, full, along_x, along_y)
    one = Ring(
        lambda p, c: along_x.at[p, :, c], here.x, here.right, here.left, (factor_send.at[0], factor_recv.at[0])
    )
    two = Ring(
        lambda p, c: along_y.at[p, :, c], here.y, here.down, here.up, (factor_send.at[1], factor_recv.at[1])
    )
    one.start()
    two.start()
    both(one, two)
    one.finish()
    two.finish()
    products(here, along_x, along_y, product)
    settle_pieces = send_pieces(here, source, product, pieces, landing, piece_send, piece_recv)

    def assemble():
        add_pieces(here, source, parent, landing, piece_recv, out)

    eliminate(here, assemble, out, panel, across, msg, corner, work, sems)
    for ring in rings + [one, two]:
        ring.settle()
    settle_pieces()


DMA = pltpu.SemaphoreType.DMA


def on_device(parent_front, child_front, inverse_factor, child_index, child_blocks):
    rows, cols = parent_front.shape
    groups, blocks = child_index.shape
    live = jnp.arange(blocks)[None, :] < child_blocks[:, None]
    kept = jnp.where(live, child_index, -1).reshape(groups, groups, 1, blocks // groups)
    slot_blocks = N // BLK // groups
    slot_ids = jnp.arange(N // BLK).reshape(1, groups, slot_blocks, 1)
    source = (kept == slot_ids).astype(jnp.float32).reshape(groups, -1)
    local, depth = child_front.shape[1:]
    shard = inverse_factor.shape[1]
    smem = pl.BlockSpec(memory_space=pltpu.SMEM)
    vmem = pl.BlockSpec(memory_space=pltpu.VMEM)
    return pl.pallas_call(
        front_kernel,
        out_shape=jax.ShapeDtypeStruct((rows, cols), jnp.float32),
        in_specs=[smem, smem, vmem, vmem, vmem],
        out_specs=vmem,
        scratch_shapes=[
            pltpu.VMEM((4, 4, shard, depth), jnp.bfloat16),
            pltpu.VMEM((4, local, depth), jnp.bfloat16),
            pltpu.VMEM((4, local, depth), jnp.bfloat16),
            pltpu.VMEM((4, 8, local, BLK), jnp.bfloat16),
            pltpu.VMEM((4, 4, local, cols), jnp.bfloat16),
            pltpu.VMEM((16, local, cols), jnp.bfloat16),
            DMA((4, 4)),
            DMA((4, 4)),
            DMA((2, 4)),
            DMA((2, 4)),
            DMA((4, 4)),
            DMA((16,)),
            pltpu.VMEM((rows, PIV_COLS), jnp.float32),
            pltpu.VMEM((PIV_COLS, cols), jnp.float32),
            pltpu.VMEM((PANELS, BLK, PIV_COLS), jnp.float32),
            pltpu.VMEM((PIV_COLS, PIV_COLS), jnp.float32),
            pltpu.VMEM((BLK, 2 * BLK), jnp.float32),
            DMA((2, CHUNKS, 4)),
            DMA((2, CHUNKS)),
            DMA((PANELS, 3)),
            DMA((PANELS,)),
            DMA((PANELS, 7)),
            DMA((PANELS,)),
        ],
        compiler_params=pltpu.CompilerParams(
            collective_id=1, has_side_effects=True, vmem_limit_bytes=56 * 1024 * 1024
        ),
        name="assemble_and_eliminate",
    )(source, live.astype(jnp.float32), parent_front, child_front, inverse_factor)


def solution(mesh):
    placed = (P("group", "dev"), P("group", "dev", None), P("group", "dev", None), P(), P())
    return jax.shard_map(
        on_device, mesh=mesh, in_specs=placed, out_specs=P("group", "dev"), check_vma=False
    )
```

```python
import jax
import jax.numpy as jnp
from jax import lax
from jax.experimental import pallas as pl
from jax.experimental.pallas import tpu as pltpu
from jax.sharding import PartitionSpec as P

N = 8192
BLK = 128
PANELS = 4
PIV_COLS = BLK * PANELS
MESH = pl.DeviceIdType.MESH
EXACT = lax.Precision.HIGHEST
STRIP = 16


def dot(a, b, contract, precision=EXACT):
    return lax.dot_general(
        a, b, (contract, ((), ())), precision=precision, preferred_element_type=jnp.float32
    )


def split(value):
    high = value.astype(jnp.bfloat16)
    return high, (value - high.astype(jnp.float32)).astype(jnp.bfloat16)


def dot_split(a, b, contract=((1,), (1,))):
    total = dot(a[0], b[1], contract, None) + dot(a[1], b[0], contract, None)
    return total + dot(a[0], b[0], contract, None)


def dot_tn(a, b):
    a, b = split(a), split(b)
    left = jnp.concatenate([a[0], a[0], a[1]], axis=0)
    right = jnp.concatenate([b[0], b[1], b[0]], axis=0)
    return dot(left, right, ((0,), (0,)), None)


class Place:
    def __init__(self):
        self.group = lax.axis_index("group")
        self.dev = lax.axis_index("dev")
        self.x = self.dev % 4
        self.y = self.dev // 4
        self.z = self.group // 2
        self.core = self.group % 2
        self.right = (self.group, self.y * 4 + (self.x + 1) % 4)
        self.left = (self.group, self.y * 4 + (self.x + 3) % 4)
        self.down = (self.group, (self.y + 1) % 4 * 4 + self.x)
        self.up = (self.group, (self.y + 3) % 4 * 4 + self.x)
        self.above = ((self.z + 1) % 4 * 2 + self.core, self.dev)
        self.below = ((self.z + 3) % 4 * 2 + self.core, self.dev)
        self.mate = (self.z * 2 + 1 - self.core, self.dev)

    def rows_first(self):
        x, y = self.x, self.y
        return [
            ((y == 0) & (x < 2), self.right),
            (((y == 0) & (x == 0)) | ((x == 1) & (y != 0)), self.left),
            ((x != 0) & (y < 2), self.down),
            ((x != 0) & (y == 0), self.up),
        ]

    def cols_first(self):
        x, y = self.x, self.y
        return [
            ((x == 0) & (y < 2), self.down),
            (((x == 0) & (y == 0)) | ((y == 1) & (x != 0)), self.up),
            ((y != 0) & (x < 2), self.right),
            ((y != 0) & (x == 0), self.left),
        ]

    def through_groups(self):
        z, core = self.z, self.core
        return [
            ((core == 0) & (z < 2), self.above),
            ((core == 0) & (z == 0), self.below),
            (core == 0, self.mate),
        ]

    def everywhere(self):
        edges = [(cond & (self.group == 0), to) for cond, to in self.rows_first()]
        return edges + self.through_groups()

    def depths(self):
        x, y = self.x, self.y

        def hops(k):
            return jnp.minimum(k, 4 - k)

        rows = jnp.where((x == 0) & (y != 0), 2 + hops(y), hops(x) + hops(y))
        cols = jnp.where((y == 0) & (x != 0), 2 + hops(x), hops(x) + hops(y))
        groups = hops(self.z) + self.core
        return rows, cols, groups, rows + groups


def remote(src, dst, send, recv, to):
    return pltpu.make_async_remote_copy(
        src_ref=src, dst_ref=dst, send_sem=send, recv_sem=recv, device_id=to, device_id_type=MESH
    )


def forward(edges, ref, sends, recv):
    for e, (cond, to) in enumerate(edges):
        @pl.when(cond)
        def _(e=e, to=to):
            remote(ref, ref, sends.at[e], recv, to).start()


def wait_sends(edges, ref, sends, recv):
    for e, (cond, to) in enumerate(edges):
        @pl.when(cond)
        def _(e=e, to=to):
            remote(ref, ref, sends.at[e], recv, to).wait_send()


def factor_block(work):
    for s in range(BLK // STRIP):
        top = s * STRIP
        strip = work[top : top + STRIP, :]
        cols = [
            jnp.broadcast_to(strip[:, top + i : top + i + 1], (STRIP, BLK)) for i in range(STRIP)
        ]
        row_id = lax.broadcasted_iota(jnp.int32, (STRIP, BLK), 0)
        for i in range(STRIP):
            root = lax.rsqrt(cols[i][i : i + 1, :])
            scaled = strip[i : i + 1, :] * jnp.concatenate([root, root], axis=1)
            under = jnp.where(row_id > i, cols[i] * root, 0.0)
            under2 = jnp.concatenate([under, under], axis=1)
            at = jnp.concatenate([row_id, row_id], axis=1) == i
            strip = jnp.where(at, scaled, strip - under2 * scaled)
            for k in range(i + 1, STRIP):
                cols[k] = cols[k] - under * (cols[k][i : i + 1, :] * root)
        work[top : top + STRIP, :] = strip
        rest = top + STRIP
        if rest < BLK:
            work[rest:, :] = work[rest:, :] - dot_tn(strip[:, rest:BLK], strip)


CHUNKS = 8
MESSAGE_TICK = 3


def chunk(ref, first, c):
    step = 64
    return ref.at[pl.ds(pl.multiple_of(first + c * step, step), step), :]


def streams(here, panel, across, sems):
    panel_send, panel_recv, across_send, across_recv = sems
    rows, cols, groups, _ = here.depths()
    half = panel.shape[0] // 2
    wanted = here.dev != 0
    zedges = [(cond & wanted, to) for cond, to in here.through_groups()]
    return [
        (here.rows_first(), lambda c: chunk(panel, 0, c), panel_send.at[0], panel_recv.at[0], rows, wanted),
        (here.cols_first(), lambda c: chunk(panel, half, c), panel_send.at[1], panel_recv.at[1], cols, wanted),
        (zedges, lambda c: chunk(across, 0, c), across_send, across_recv, groups, wanted & (here.group != 0)),
    ]


def move(stream, c, wait):
    edges, ref, send, recv, _, incoming = stream
    if wait:
        @pl.when(incoming)
        def _():
            remote(ref(c), ref(c), recv.at[c], recv.at[c], edges[0][1]).wait_recv()

    forward(edges, ref(c), send.at[c], recv.at[c])


def settle_streams(all_streams):
    for edges, ref, send, recv, _, _ in all_streams:
        def done(c, _):
            wait_sends(edges, ref(c), send.at[c], recv.at[c])
            return 0

        lax.fori_loop(0, CHUNKS, done, 0)


def diagonal_ref(msg, k):
    return msg.at[k * BLK : (k + 1) * BLK, k * BLK : (k + 1) * BLK]


def before_ref(msg, k):
    return msg.at[k * BLK : (k + 1) * BLK, 0 : k * BLK]


def messages(msg):
    refs = [diagonal_ref(msg, 0)]
    for k in range(1, PANELS):
        refs += [before_ref(msg, k), diagonal_ref(msg, k)]
    return refs


def inverse_row(inv, msg, k):
    low, high = k * BLK, (k + 1) * BLK
    inv[low:high, low:high] = msg[low:high, low:high]
    if k > 0:
        inv[low:high, 0:low] = -dot(msg[low:high, low:high], msg[low:high, 0:low], ((1,), (0,)))


def factor_corner(corner, msg, inv, work, every, sems):
    send, recv = sems
    diag = lax.broadcasted_iota(jnp.int32, (BLK, BLK), 0) - lax.broadcasted_iota(jnp.int32, (BLK, BLK), 1)

    def one_panel(k, _):
        for kk in range(PANELS):
            @pl.when(k == kk)
            def _():
                work[:, 0:BLK] = corner[kk * BLK : (kk + 1) * BLK, kk * BLK : (kk + 1) * BLK]

        work[:, BLK:] = jnp.where(diag == 0, 1.0, 0.0)
        factor_block(work)
        inverse = jnp.where(diag >= 0, work[:, BLK:], 0.0)
        for kk in range(PANELS):
            @pl.when(k == kk)
            def _():
                low, high = kk * BLK, (kk + 1) * BLK
                msg[low:high, low:high] = inverse
                forward(every, diagonal_ref(msg, kk), send.at[2 * kk], recv.at[2 * kk])
                if kk < PANELS - 1:
                    strip = dot(inverse, corner[low:high, high:], ((1,), (0,)))
                    corner[low:high, high:] = strip
                    corner[high:, high:] = corner[high:, high:] - dot_tn(strip, strip)
                inverse_row(inv, msg, kk)
                if kk < PANELS - 1:
                    end = high + BLK
                    msg[high:end, 0:high] = dot(corner[0:high, high:end], inv[0:high, 0:high], ((0,), (0,)))
                    forward(every, before_ref(msg, kk + 1), send.at[2 * kk + 1], recv.at[2 * kk + 1])
                corner[low:high, low:high] = jnp.where(diag <= 0, work[:, 0:BLK], 0.0)

        return 0

    lax.fori_loop(0, PANELS, one_panel, 0)


STEP = 2 * BLK


def solve_rows(here, out, panel, across, tall, wide, inv):
    inverse = split(inv[...])

    def one(p, _):
        at = pl.ds(pl.multiple_of(p * STEP, STEP), STEP)
        solved = dot_split(split(panel[at, :]), inverse)
        tall[0, at, :], tall[1, at, :] = split(solved)

        @pl.when(here.dev == 0)
        def _():
            out[at, :] = solved

        return 0

    lax.fori_loop(0, panel.shape[0] // STEP, one, 0)

    @pl.when(here.dev != 0)
    def _():
        for low in range(0, across.shape[1], STEP):
            at = slice(low, low + STEP)
            wide[0, at, :], wide[1, at, :] = split(dot_split(split(across[:, at]), inverse, ((0,), (1,))))


def update_tile(out, tall, wide):
    def one(p, _):
        at = pl.ds(pl.multiple_of(p * STEP, STEP), STEP)
        out[at, :] = out[at, :] - dot_split((tall[0, at, :], tall[1, at, :]), (wide[0], wide[1]))
        return 0

    lax.fori_loop(0, out.shape[0] // STEP, one, 0)


def eliminate(here, out, panel, across, tall, wide, msg, inv, corner, work, sems):
    msg_send, msg_recv = sems[4:6]
    group, dev = here.group, here.dev
    first = (group == 0) & (dev == 0)
    later = jnp.logical_not(first)
    every = here.everywhere()
    refs = messages(msg)
    chunked = streams(here, panel, across, sems[0:4])
    depth = here.depths()[3]

    @pl.when(dev == 0)
    def _():
        panel[...] = out[...]

    @pl.when(group == 0)
    def _():
        across[...] = out[0:PIV_COLS, :]

    for k in range(PANELS - 1):
        inv[k * BLK : (k + 1) * BLK, (k + 1) * BLK :] = jnp.zeros((BLK, PIV_COLS - (k + 1) * BLK), jnp.float32)

    @pl.when(first)
    def _():
        def start(c, _):
            for stream in chunked:
                move(stream, c, False)
            return 0

        lax.fori_loop(0, CHUNKS, start, 0)
        corner[...] = out[0:PIV_COLS, :]
        factor_corner(corner, msg, inv, work, every, (msg_send, msg_recv))
        solve_rows(here, out, panel, across, tall, wide, inv)
        out[0:PIV_COLS, :] = jnp.zeros((PIV_COLS, PIV_COLS), jnp.float32)
        for k in range(PANELS):
            for i in range(k, PANELS):
                rows, cols = slice(i * BLK, (i + 1) * BLK), slice(k * BLK, (k + 1) * BLK)
                out[rows, cols] = corner[cols, rows].T

    @pl.when(later)
    def _():
        def tick(t, _):
            for stream in chunked:
                c = t - stream[4]

                @pl.when((c >= 0) & (c < CHUNKS))
                def _():
                    move(stream, c, True)

            for m, ref in enumerate(refs):
                @pl.when(t - depth - MESSAGE_TICK == m)
                def _():
                    remote(ref, ref, msg_recv.at[m], msg_recv.at[m], here.left).wait_recv()
                    forward(every, ref, msg_send.at[m], msg_recv.at[m])

            return 0

        lax.fori_loop(0, MESSAGE_TICK + 8 + len(refs), tick, 0)
        for k in range(PANELS):
            inverse_row(inv, msg, k)
        solve_rows(here, out, panel, across, tall, wide, inv)

        @pl.when(dev != 0)
        def _():
            update_tile(out, tall, wide)

    @pl.when((group == 0) & (dev != 0))
    def _():
        out[0:PIV_COLS, :] = jnp.zeros((PIV_COLS, PIV_COLS), jnp.float32)

    settle_streams(chunked)
    for m, ref in enumerate(refs):
        wait_sends(every, ref, msg_send.at[m], msg_recv.at[m])


class Ring:
    def __init__(self, region, me, after, before, sems):
        self.after, self.before = after, before
        self.send, self.recv = sems
        width = region(me, slice(None)).shape[-1]
        low, high = slice(0, width // 2), slice(width // 2, width)
        self.own = region(me, slice(None))
        self.prev, self.next = region((me + 3) % 4, slice(None)), region((me + 1) % 4, slice(None))
        self.relays = region((me + 3) % 4, low), region((me + 1) % 4, high)
        self.far = region((me + 2) % 4, low), region((me + 2) % 4, high)

    def copy(self, ref, k, to):
        return remote(ref, ref, self.send.at[k], self.recv.at[k], to)

    def start(self):
        self.copy(self.own, 0, self.after).start()
        self.copy(self.own, 1, self.before).start()

    def relay_prev(self):
        self.copy(self.prev, 0, self.after).wait_recv()
        self.copy(self.relays[0], 2, self.after).start()

    def relay_next(self):
        self.copy(self.next, 1, self.before).wait_recv()
        self.copy(self.relays[1], 3, self.before).start()

    def finish(self):
        self.copy(self.far[0], 2, self.after).wait_recv()
        self.copy(self.far[1], 3, self.before).wait_recv()

    def settle(self):
        self.copy(self.own, 0, self.after).wait_send()
        self.copy(self.own, 1, self.before).wait_send()
        self.copy(self.relays[0], 2, self.after).wait_send()
        self.copy(self.relays[1], 3, self.before).wait_send()


def both(one, two):
    for step in ("relay_prev", "relay_next"):
        getattr(one, step)()
        getattr(two, step)()


def gather_plane(here, full, sems):
    send, recv = sems
    rows = full.shape[2]
    low, high = slice(0, rows // 2), slice(rows // 2, rows)
    between = (slice(None),) * (len(full.shape) - 4)
    x, y = here.x, here.y

    def ring(region, me, after, before, k):
        return Ring(region, me, after, before, (send.at[k], recv.at[k]))

    def at(*index):
        return full.at[index[:3] + between + index[3:]]

    one = ring(lambda p, c: at(y, p, low, c), x, here.right, here.left, 0)
    two = ring(lambda p, c: at(p, x, high, c), y, here.down, here.up, 1)
    three = ring(lambda p, c: at(p, slice(None), low, c), y, here.down, here.up, 2)
    four = ring(lambda p, c: at(slice(None), p, high, c), x, here.right, here.left, 3)
    one.start()
    two.start()
    both(one, two)
    one.finish()
    three.start()
    two.finish()
    four.start()
    both(three, four)
    three.finish()
    four.finish()
    return [one, two, three, four]


def child_factor(here, live, front, full, along_x, along_y):
    rows = front.shape[1]
    depth = full.shape[3]
    step = 512
    for low in range(0, depth, step):
        total = jnp.zeros((rows, step), jnp.float32)
        for k in range(4):
            share = full[k, :, :, low : low + step].reshape(depth // 4, step)
            total += dot(front[0, :, k * (depth // 4) : (k + 1) * (depth // 4)], share, ((1,), (0,)), None)
        for b in range(rows // BLK):
            part = slice(b * BLK, (b + 1) * BLK)
            scale = live[here.group, here.dev * (rows // BLK) + b]
            factor = (total[part] * scale).astype(jnp.bfloat16)
            along_x[here.x, part, low : low + step] = factor
            along_y[here.y, part, low : low + step] = factor


def products(here, along_x, along_y, product):
    def one(k, _):
        rows = along_y[k]
        for p in range(4):
            value = dot(rows, along_x[p], ((1,), (1,)), None).astype(jnp.bfloat16)
            product[k, 2 * p] = value[:, 0:BLK]
            product[k, 2 * p + 1] = value[:, BLK:]
        return 0

    lax.fori_loop(0, 4, one, 0)


def expand(here, source, product, to_z, to_x, j):
    at = ((4 * here.y + to_x) * 4 + j) * 4
    total = jnp.zeros(product.shape[2:], jnp.float32)
    for i in range(4):
        total += product[to_z, to_x // 2 * 4 + i].astype(jnp.float32) * source[here.group, at + i]
    return total


def send_pieces(here, source, product, pieces, landing, send, recv):
    x, y, z, group = here.x, here.y, here.z, here.group
    slot = group * 2 + x % 2
    urgent = (y == 0) & (x < 2)

    def visit(to_x, to_z, act):
        target = (to_z * 2 + x // 2, y * 4 + to_x)
        own = (target[0] == group) & (to_x == x)
        copy = remote(pieces.at[to_z, to_x], landing.at[slot], send.at[to_z, to_x], recv.at[slot], target)
        act(to_x, to_z, own, copy)

    def start(to_x, to_z, own, copy):
        for j in range(4):
            total = expand(here, source, product, to_z, to_x, j)
            pieces[to_z, to_x, :, j * BLK : (j + 1) * BLK] = total.astype(jnp.bfloat16)

        @pl.when(own)
        def _():
            landing[slot] = pieces[to_z, to_x]

        @pl.when(jnp.logical_not(own))
        def _():
            copy.start()

    def relative(step):
        return (x + step // 4) % 4, (z + step) % 4

    @pl.when(urgent)
    def _():
        visit(0, 0, start)

    def one(step, _):
        to_x, to_z = relative(step)

        @pl.when(jnp.logical_not(urgent & (to_x == 0) & (to_z == 0)))
        def _():
            visit(to_x, to_z, start)

        return 0

    lax.fori_loop(0, 16, one, 0)

    def settle():
        def finish(to_x, to_z, own, copy):
            @pl.when(jnp.logical_not(own))
            def _():
                copy.wait_send()

        def done(step, _):
            visit(*relative(step), finish)
            return 0

        lax.fori_loop(0, 16, done, 0)

    return settle


def sources(here):
    return [
        (g * 2 + p, (g, here.y * 4 + here.core * 2 + p), (here.group == g) & (here.x == here.core * 2 + p))
        for g in range(8)
        for p in range(2)
    ]


def add_pieces(here, source, parent, landing, recv, out):
    group = here.group

    for slot, _, own in sources(here):
        @pl.when(jnp.logical_not(own))
        def _():
            ref = landing.at[slot]
            remote(ref, ref, recv.at[slot], recv.at[slot], here.mate).wait_recv()

    step = 32

    def one(k, _):
        q, r = k // 4, k % 4
        at = pl.ds(pl.multiple_of(k * step, step), step)
        total = jnp.zeros((step, out.shape[1]), jnp.float32)
        for g in range(8):
            for i in range(4):
                row = pl.ds(pl.multiple_of(i % 2 * BLK + r * step, step), step)
                piece = landing[g * 2 + i // 2, row, :].astype(jnp.float32)
                total += piece * source[g, (group * 8 + q) * 4 + i]
        out[at, :] = parent[at, :] - total
        return 0

    lax.fori_loop(0, out.shape[0] // step, one, 0)


def signal(to, cond=None):
    barrier = pltpu.get_barrier_semaphore()
    if cond is None:
        pl.semaphore_signal(barrier, inc=1, device_id=to, device_id_type=MESH)
    else:
        @pl.when(cond)
        def _():
            pl.semaphore_signal(barrier, inc=1, device_id=to, device_id_type=MESH)


def greet(here):
    x, core = here.x, here.core
    for to in [here.right, here.left, here.down, here.up, here.above, here.below, here.mate]:
        signal(to)
    for _, to, own in sources(here):
        signal(to, jnp.logical_not(own))
    pl.semaphore_wait(pltpu.get_barrier_semaphore(), jnp.where(core == x // 2, 22, 23))


def front_kernel(
    source, live, parent, front, inverse, out,
    full, along_x, along_y, product, pieces, landing,
    inverse_send, inverse_recv, factor_send, factor_recv, piece_send, piece_recv,
    panel, across, tall, wide, msg, inv, corner, work, *sems
):
    here = Place()
    greet(here)
    full[here.y, here.x] = inverse[0]
    rings = gather_plane(here, full, (inverse_send, inverse_recv))
    child_factor(here, live, front, full, along_x, along_y)
    one = Ring(
        lambda p, c: along_x.at[p, :, c], here.x, here.right, here.left, (factor_send.at[0], factor_recv.at[0])
    )
    two = Ring(
        lambda p, c: along_y.at[p, :, c], here.y, here.down, here.up, (factor_send.at[1], factor_recv.at[1])
    )
    one.start()
    two.start()
    both(one, two)
    one.finish()
    two.finish()
    products(here, along_x, along_y, product)

    settle_pieces = send_pieces(here, source, product, pieces, landing, piece_send, piece_recv)

    add_pieces(here, source, parent, landing, piece_recv, out)
    eliminate(here, out, panel, across, tall, wide, msg, inv, corner, work, sems)
    for ring in rings + [one, two]:
        ring.settle()
    settle_pieces()


DMA = pltpu.SemaphoreType.DMA


def on_device(parent_front, child_front, inverse_factor, child_index, child_blocks):
    rows, cols = parent_front.shape
    groups, blocks = child_index.shape
    live = jnp.arange(blocks)[None, :] < child_blocks[:, None]
    kept = jnp.where(live, child_index, -1).reshape(groups, groups, 1, blocks // groups)
    slot_blocks = N // BLK // groups
    slot_ids = jnp.arange(N // BLK).reshape(1, groups, slot_blocks, 1)
    source = (kept == slot_ids).astype(jnp.float32).reshape(groups, -1)
    local, depth = child_front.shape[1:]
    shard = inverse_factor.shape[1]
    smem = pl.BlockSpec(memory_space=pltpu.SMEM)
    vmem = pl.BlockSpec(memory_space=pltpu.VMEM)
    return pl.pallas_call(
        front_kernel,
        out_shape=jax.ShapeDtypeStruct((rows, cols), jnp.float32),
        in_specs=[smem, smem, vmem, vmem, vmem],
        out_specs=vmem,
        scratch_shapes=[
            pltpu.VMEM((4, 4, shard, depth), jnp.bfloat16),
            pltpu.VMEM((4, local, depth), jnp.bfloat16),
            pltpu.VMEM((4, local, depth), jnp.bfloat16),
            pltpu.VMEM((4, 8, local, BLK), jnp.bfloat16),
            pltpu.VMEM((4, 4, local, cols), jnp.bfloat16),
            pltpu.VMEM((16, local, cols), jnp.bfloat16),
            DMA((4, 4)),
            DMA((4, 4)),
            DMA((2, 4)),
            DMA((2, 4)),
            DMA((4, 4)),
            DMA((16,)),
            pltpu.VMEM((rows, PIV_COLS), jnp.float32),
            pltpu.VMEM((PIV_COLS, cols), jnp.float32),
            pltpu.VMEM((2, rows, PIV_COLS), jnp.bfloat16),
            pltpu.VMEM((2, cols, PIV_COLS), jnp.bfloat16),
            pltpu.VMEM((PIV_COLS, PIV_COLS), jnp.float32),
            pltpu.VMEM((PIV_COLS, PIV_COLS), jnp.float32),
            pltpu.VMEM((PIV_COLS, PIV_COLS), jnp.float32),
            pltpu.VMEM((BLK, 2 * BLK), jnp.float32),
            DMA((2, CHUNKS, 4)),
            DMA((2, CHUNKS)),
            DMA((CHUNKS, 3)),
            DMA((CHUNKS,)),
            DMA((2 * PANELS - 1, 7)),
            DMA((2 * PANELS - 1,)),
        ],
        compiler_params=pltpu.CompilerParams(
            collective_id=1, has_side_effects=True, vmem_limit_bytes=56 * 1024 * 1024
        ),
        name="assemble_and_eliminate",
    )(source, live.astype(jnp.float32), parent_front, child_front, inverse_factor)


def solution(mesh):
    placed = (P("group", "dev"), P("group", "dev", None), P("group", "dev", None), P(), P())
    return jax.shard_map(
        on_device, mesh=mesh, in_specs=placed, out_specs=P("group", "dev"), check_vma=False
    )
```

```python
import functools

import jax
import jax.numpy as jnp
from jax import lax
from jax.experimental import pallas as pl
from jax.experimental.pallas import tpu as pltpu
from jax.sharding import PartitionSpec as P

N = 8192
BLK = 128
PANELS = 4
PIV_COLS = BLK * PANELS
MESH = pl.DeviceIdType.MESH
EXACT = lax.Precision.HIGHEST
STRIP = 16


def dot(a, b, contract, precision=EXACT):
    return lax.dot_general(
        a, b, (contract, ((), ())), precision=precision, preferred_element_type=jnp.float32
    )


def split(value):
    high = value.astype(jnp.bfloat16)
    return high, (value - high.astype(jnp.float32)).astype(jnp.bfloat16)


def dot_split(a, b, contract=((1,), (1,))):
    total = dot(a[0], b[1], contract, None) + dot(a[1], b[0], contract, None)
    return total + dot(a[0], b[0], contract, None)


def dot_tn(a, b):
    a, b = split(a), split(b)
    left = jnp.concatenate([a[0], a[0], a[1]], axis=0)
    right = jnp.concatenate([b[0], b[1], b[0]], axis=0)
    return dot(left, right, ((0,), (0,)), None)


TREES = (
    ((26183, 6, 8736, 8194), (65534, 65532, 57304, 36224, 2048)),
    ((48, 3953, 272, 224), (65534, 65518, 65102, 58372, 16384)),
    ((34944, 136, 19661, 12), (65534, 65526, 32626, 10016, 512)),
    ((4352, 57344, 36864, 57089), (65534, 61438, 20222, 1252, 64)),
)
TREE_DEPTH = 5


class Place:
    def __init__(self):
        self.group = lax.axis_index("group")
        self.dev = lax.axis_index("dev")
        self.x = self.dev % 4
        self.y = self.dev // 4
        self.z = self.group // 2
        self.core = self.group % 2
        self.right = (self.group, self.y * 4 + (self.x + 1) % 4)
        self.left = (self.group, self.y * 4 + (self.x + 3) % 4)
        self.down = (self.group, (self.y + 1) % 4 * 4 + self.x)
        self.up = (self.group, (self.y + 3) % 4 * 4 + self.x)
        self.above = ((self.z + 1) % 4 * 2 + self.core, self.dev)
        self.below = ((self.z + 3) % 4 * 2 + self.core, self.dev)
        self.mate = (self.z * 2 + 1 - self.core, self.dev)

    def within(self, mask):
        return (jnp.int32(mask) >> self.dev) & 1

    def tree(self, k):
        ways = (self.right, self.down, self.left, self.up)
        return [(self.within(mask) == 1, to) for mask, to in zip(TREES[k][0], ways)]

    def tree_depth(self, k):
        return sum(self.within(mask) for mask in TREES[k][1])

    def through_groups(self):
        z, core = self.z, self.core
        return [
            ((core == 0) & (z < 2), self.above),
            ((core == 0) & (z == 0), self.below),
            (core == 0, self.mate),
        ]

    def everywhere(self):
        x, y, lead = self.x, self.y, self.group == 0
        return [
            (lead & (y == 0) & (x < 2), self.right),
            (lead & (y == 0) & (x == 0), self.left),
            (lead & (y < 2), self.down),
            (lead & (y == 0), self.up),
        ] + self.through_groups()

    def hops(self):
        def ring(k):
            return jnp.minimum(k, 4 - k)

        groups = ring(self.z) + self.core
        return groups, groups + ring(self.x) + ring(self.y)


def remote(src, dst, send, recv, to):
    return pltpu.make_async_remote_copy(
        src_ref=src, dst_ref=dst, send_sem=send, recv_sem=recv, device_id=to, device_id_type=MESH
    )


def forward(edges, ref, sends, recv):
    for e, (cond, to) in enumerate(edges):
        @pl.when(cond)
        def _(e=e, to=to):
            remote(ref, ref, sends.at[e], recv, to).start()


def wait_sends(edges, ref, sends, recv):
    for e, (cond, to) in enumerate(edges):
        @pl.when(cond)
        def _(e=e, to=to):
            remote(ref, ref, sends.at[e], recv, to).wait_send()


def factor_block(work):
    for s in range(BLK // STRIP):
        top = s * STRIP
        strip = work[top : top + STRIP, :]
        cols = [
            jnp.broadcast_to(strip[:, top + i : top + i + 1], (STRIP, BLK)) for i in range(STRIP)
        ]
        row_id = lax.broadcasted_iota(jnp.int32, (STRIP, BLK), 0)
        for i in range(STRIP):
            root = lax.rsqrt(cols[i][i : i + 1, :])
            scaled = strip[i : i + 1, :] * jnp.concatenate([root, root], axis=1)
            under = jnp.where(row_id > i, cols[i] * root, 0.0)
            under2 = jnp.concatenate([under, under], axis=1)
            at = jnp.concatenate([row_id, row_id], axis=1) == i
            strip = jnp.where(at, scaled, strip - under2 * scaled)
            for k in range(i + 1, STRIP):
                cols[k] = cols[k] - under * (cols[k][i : i + 1, :] * root)
        work[top : top + STRIP, :] = strip
        rest = top + STRIP
        if rest < BLK:
            work[rest:, :] = work[rest:, :] - dot_tn(strip[:, rest:BLK], strip)


CHUNKS = 4
HOP_TICKS = 2


def chunk(ref, first, step, c):
    return ref.at[pl.ds(pl.multiple_of(first + c * step, step), step), :]


def streams(here, panel, across, sems):
    panel_send, panel_recv, across_send, across_recv = sems
    part = panel.shape[0] // 4
    wanted = here.dev != 0
    zedges = [(cond & wanted, to) for cond, to in here.through_groups()]
    result = []
    for k in range(4):
        ref = functools.partial(chunk, panel, k * part, part // CHUNKS)
        result.append((here.tree(k), ref, panel_send.at[k], panel_recv.at[k], here.tree_depth(k), wanted))
    ref = functools.partial(chunk, across, 0, across.shape[0] // CHUNKS)
    result.append((zedges, ref, across_send, across_recv, here.hops()[0], wanted & (here.group != 0)))
    return result


def move(stream, c, wait):
    edges, ref, send, recv, _, incoming = stream
    if wait:
        @pl.when(incoming)
        def _():
            remote(ref(c), ref(c), recv.at[c], recv.at[c], edges[0][1]).wait_recv()

    forward(edges, ref(c), send.at[c], recv.at[c])


def settle_streams(all_streams):
    for edges, ref, send, recv, _, _ in all_streams:
        def done(c, _):
            wait_sends(edges, ref(c), send.at[c], recv.at[c])
            return 0

        lax.fori_loop(0, CHUNKS, done, 0)


def diagonal_ref(msg, k):
    return msg.at[k * BLK : (k + 1) * BLK, k * BLK : (k + 1) * BLK]


def before_ref(msg, k):
    return msg.at[k * BLK : (k + 1) * BLK, 0 : k * BLK]


def messages(msg):
    refs = [diagonal_ref(msg, 0)]
    for k in range(1, PANELS):
        refs += [before_ref(msg, k), diagonal_ref(msg, k)]
    return refs


def inverse_row(inv, msg, k):
    low, high = k * BLK, (k + 1) * BLK
    inv[low:high, low:high] = msg[low:high, low:high]
    if k > 0:
        inv[low:high, 0:low] = -dot_split(split(msg[low:high, low:high]), split(msg[low:high, 0:low]), ((1,), (0,)))


def factor_corner(corner, msg, inv, work, every, sems):
    send, recv = sems
    diag = lax.broadcasted_iota(jnp.int32, (BLK, BLK), 0) - lax.broadcasted_iota(jnp.int32, (BLK, BLK), 1)

    def one_panel(k, _):
        for kk in range(PANELS):
            @pl.when(k == kk)
            def _():
                work[:, 0:BLK] = corner[kk * BLK : (kk + 1) * BLK, kk * BLK : (kk + 1) * BLK]

        work[:, BLK:] = jnp.where(diag == 0, 1.0, 0.0)
        factor_block(work)
        inverse = jnp.where(diag >= 0, work[:, BLK:], 0.0)
        for kk in range(PANELS):
            @pl.when(k == kk)
            def _():
                low, high = kk * BLK, (kk + 1) * BLK
                msg[low:high, low:high] = inverse
                forward(every, diagonal_ref(msg, kk), send.at[2 * kk], recv.at[2 * kk])
                if kk < PANELS - 1:
                    strip = dot(inverse, corner[low:high, high:], ((1,), (0,)))
                    corner[low:high, high:] = strip
                    corner[high:, high:] = corner[high:, high:] - dot_tn(strip, strip)
                inverse_row(inv, msg, kk)
                if kk < PANELS - 1:
                    end = high + BLK
                    msg[high:end, 0:high] = dot(corner[0:high, high:end], inv[0:high, 0:high], ((0,), (0,)))
                    forward(every, before_ref(msg, kk + 1), send.at[2 * kk + 1], recv.at[2 * kk + 1])
                corner[low:high, low:high] = jnp.where(diag <= 0, work[:, 0:BLK], 0.0)

        return 0

    lax.fori_loop(0, PANELS, one_panel, 0)


STEP = 2 * BLK


def solve_rows(here, out, panel, across, tall, wide, inv):
    inverse = split(inv[...])

    def one(p, _):
        at = pl.ds(pl.multiple_of(p * STEP, STEP), STEP)
        solved = dot_split(split(panel[at, :]), inverse)
        tall[0, at, :], tall[1, at, :] = split(solved)

        @pl.when(here.dev == 0)
        def _():
            out[at, :] = solved

        return 0

    lax.fori_loop(0, panel.shape[0] // STEP, one, 0)

    @pl.when(here.dev != 0)
    def _():
        for low in range(0, across.shape[1], STEP):
            at = slice(low, low + STEP)
            wide[0, at, :], wide[1, at, :] = split(dot_split(split(across[:, at]), inverse, ((0,), (1,))))


def update_tile(out, tall, wide):
    def one(p, _):
        at = pl.ds(pl.multiple_of(p * STEP, STEP), STEP)
        out[at, :] = out[at, :] - dot_split((tall[0, at, :], tall[1, at, :]), (wide[0], wide[1]))
        return 0

    lax.fori_loop(0, out.shape[0] // STEP, one, 0)


def eliminate(here, out, panel, across, tall, wide, msg, inv, corner, work, sems):
    msg_send, msg_recv = sems[4:6]
    group, dev = here.group, here.dev
    first = (group == 0) & (dev == 0)
    later = jnp.logical_not(first)
    every = here.everywhere()
    refs = messages(msg)
    chunked = streams(here, panel, across, sems[0:4])
    depth = here.hops()[1]

    @pl.when(dev == 0)
    def _():
        panel[...] = out[...]

    @pl.when(group == 0)
    def _():
        across[...] = out[0:PIV_COLS, :]

    for k in range(PANELS - 1):
        inv[k * BLK : (k + 1) * BLK, (k + 1) * BLK :] = jnp.zeros((BLK, PIV_COLS - (k + 1) * BLK), jnp.float32)

    @pl.when(first)
    def _():
        def start(c, _):
            for stream in chunked:
                move(stream, c, False)
            return 0

        lax.fori_loop(0, CHUNKS, start, 0)
        corner[...] = out[0:PIV_COLS, :]
        factor_corner(corner, msg, inv, work, every, (msg_send, msg_recv))
        solve_rows(here, out, panel, across, tall, wide, inv)
        out[0:PIV_COLS, :] = jnp.zeros((PIV_COLS, PIV_COLS), jnp.float32)
        for k in range(PANELS):
            for i in range(k, PANELS):
                rows, cols = slice(i * BLK, (i + 1) * BLK), slice(k * BLK, (k + 1) * BLK)
                out[rows, cols] = corner[cols, rows].T

    @pl.when(later)
    def _():
        def tick(t, _):
            for stream in chunked:
                c = t - HOP_TICKS * stream[4]

                @pl.when((c >= 0) & (c < CHUNKS))
                def _():
                    move(stream, c, True)

            for m, ref in enumerate(refs):
                @pl.when(t - HOP_TICKS * depth == m // 2)
                def _():
                    remote(ref, ref, msg_recv.at[m], msg_recv.at[m], here.left).wait_recv()
                    forward(every, ref, msg_send.at[m], msg_recv.at[m])

            return 0

        lax.fori_loop(0, max(CHUNKS + HOP_TICKS * TREE_DEPTH, HOP_TICKS * 7 + PANELS), tick, 0)
        for k in range(PANELS):
            inverse_row(inv, msg, k)
        solve_rows(here, out, panel, across, tall, wide, inv)

        @pl.when(dev != 0)
        def _():
            update_tile(out, tall, wide)

    @pl.when((group == 0) & (dev != 0))
    def _():
        out[0:PIV_COLS, :] = jnp.zeros((PIV_COLS, PIV_COLS), jnp.float32)

    settle_streams(chunked)
    for m, ref in enumerate(refs):
        wait_sends(every, ref, msg_send.at[m], msg_recv.at[m])


class Ring:
    def __init__(self, region, me, after, before, sems):
        self.after, self.before = after, before
        self.send, self.recv = sems
        width = region(me, slice(None)).shape[-1]
        low, high = slice(0, width // 2), slice(width // 2, width)
        self.own = region(me, slice(None))
        self.prev, self.next = region((me + 3) % 4, slice(None)), region((me + 1) % 4, slice(None))
        self.relays = region((me + 3) % 4, low), region((me + 1) % 4, high)
        self.far = region((me + 2) % 4, low), region((me + 2) % 4, high)

    def copy(self, ref, k, to):
        return remote(ref, ref, self.send.at[k], self.recv.at[k], to)

    def start(self):
        self.copy(self.own, 0, self.after).start()
        self.copy(self.own, 1, self.before).start()

    def relay_prev(self):
        self.copy(self.prev, 0, self.after).wait_recv()
        self.copy(self.relays[0], 2, self.after).start()

    def relay_next(self):
        self.copy(self.next, 1, self.before).wait_recv()
        self.copy(self.relays[1], 3, self.before).start()

    def finish(self):
        self.copy(self.far[0], 2, self.after).wait_recv()
        self.copy(self.far[1], 3, self.before).wait_recv()

    def settle(self):
        self.copy(self.own, 0, self.after).wait_send()
        self.copy(self.own, 1, self.before).wait_send()
        self.copy(self.relays[0], 2, self.after).wait_send()
        self.copy(self.relays[1], 3, self.before).wait_send()


def both(one, two):
    for step in ("relay_prev", "relay_next"):
        getattr(one, step)()
        getattr(two, step)()


def gather_plane(here, full, sems):
    send, recv = sems
    rows = full.shape[2]
    low, high = slice(0, rows // 2), slice(rows // 2, rows)
    between = (slice(None),) * (len(full.shape) - 4)
    x, y = here.x, here.y

    def ring(region, me, after, before, k):
        return Ring(region, me, after, before, (send.at[k], recv.at[k]))

    def at(*index):
        return full.at[index[:3] + between + index[3:]]

    one = ring(lambda p, c: at(y, p, low, c), x, here.right, here.left, 0)
    two = ring(lambda p, c: at(p, x, high, c), y, here.down, here.up, 1)
    three = ring(lambda p, c: at(p, slice(None), low, c), y, here.down, here.up, 2)
    four = ring(lambda p, c: at(slice(None), p, high, c), x, here.right, here.left, 3)
    one.start()
    two.start()
    both(one, two)
    one.finish()
    three.start()
    two.finish()
    four.start()
    both(three, four)
    three.finish()
    four.finish()
    return [one, two, three, four]


def child_factor(here, front, full, along_x, along_y):
    rows = front.shape[1]
    depth = full.shape[3]
    step = 512
    for low in range(0, depth, step):
        total = jnp.zeros((rows, step), jnp.float32)
        for k in range(4):
            share = full[k, :, :, low : low + step].reshape(depth // 4, step)
            total += dot(front[0, :, k * (depth // 4) : (k + 1) * (depth // 4)], share, ((1,), (0,)), None)
        factor = total.astype(jnp.bfloat16)
        along_x[here.x, :, low : low + step] = factor
        along_y[here.y, :, low : low + step] = factor


def multiply(along_x, along_y, product, k):
    rows = along_y[k]
    for p in range(4):
        value = dot(rows, along_x[p], ((1,), (1,)), None).astype(jnp.bfloat16)
        product[k, 2 * p] = value[:, 0:BLK]
        product[k, 2 * p + 1] = value[:, BLK:]


def expand(here, source, product, to_z, to_x, j):
    at = ((4 * here.y + to_x) * 4 + j) * 4
    total = jnp.zeros(product.shape[2:], jnp.float32)
    for i in range(4):
        total += product[to_z, to_x // 2 * 4 + i].astype(jnp.float32) * source[here.group, at + i]
    return total


def send_pieces(here, source, along_x, along_y, product, pieces, landing, send, recv):
    x, y, z, group = here.x, here.y, here.z, here.group
    slot = group * 2 + x % 2

    def visit(to_x, to_z, act):
        target = (to_z * 2 + x // 2, y * 4 + to_x)
        own = (target[0] == group) & (to_x == x)
        copy = remote(pieces.at[to_z, to_x], landing.at[slot], send.at[to_z, to_x], recv.at[slot], target)
        act(to_x, to_z, own, copy)

    def start(to_x, to_z, own, copy):
        for j in range(4):
            total = expand(here, source, product, to_z, to_x, j)
            pieces[to_z, to_x, :, j * BLK : (j + 1) * BLK] = total.astype(jnp.bfloat16)

        @pl.when(own)
        def _():
            landing[slot] = pieces[to_z, to_x]

        @pl.when(jnp.logical_not(own))
        def _():
            copy.start()

    def relative(step):
        return (x + step) % 4, (z + step // 4) % 4

    def one(step, _):
        to_x, to_z = relative(step)

        visit(to_x, to_z, start)

        return 0

    def row(j, _):
        multiply(along_x, along_y, product, (z + j) % 4)
        return lax.fori_loop(4 * j, 4 * j + 4, one, 0)

    lax.fori_loop(0, 4, row, 0)

    def settle():
        def finish(to_x, to_z, own, copy):
            @pl.when(jnp.logical_not(own))
            def _():
                copy.wait_send()

        def done(step, _):
            visit(*relative(step), finish)
            return 0

        lax.fori_loop(0, 16, done, 0)

    return settle


def sources(here):
    return [
        (g * 2 + p, (g, here.y * 4 + here.core * 2 + p), (here.group == g) & (here.x == here.core * 2 + p))
        for g in range(8)
        for p in range(2)
    ]


def add_pieces(here, source, parent, landing, recv, out):
    x, z, core, group = here.x, here.z, here.core, here.group
    near = jnp.where((x - core * 2) % 4 < (x - core * 2 - 1) % 4, 0, 1)
    step = 32
    out[...] = parent[...]

    def phase(n, _):
        p = (near + n) % 2
        z_from = (z - n // 2) % 4
        slots = [(z_from * 2 + c) * 2 + p for c in range(2)]
        for c in range(2):
            @pl.when(jnp.logical_not((z_from * 2 + c == group) & (core * 2 + p == x)))
            def _():
                ref = landing.at[slots[c]]
                remote(ref, ref, recv.at[slots[c]], recv.at[slots[c]], here.mate).wait_recv()

        def one(k, _):
            q, r = k // 4, k % 4
            at = pl.ds(pl.multiple_of(k * step, step), step)
            total = out[at, :]
            for c in range(2):
                for b in range(2):
                    row = pl.ds(pl.multiple_of(b * BLK + r * step, step), step)
                    weight = source[z_from * 2 + c, (group * 8 + q) * 4 + p * 2 + b]
                    total = total - landing[slots[c], row, :].astype(jnp.float32) * weight
            out[at, :] = total
            return 0

        lax.fori_loop(0, out.shape[0] // step, one, 0)
        return 0

    lax.fori_loop(0, 8, phase, 0)


def signal(to, cond=None):
    barrier = pltpu.get_barrier_semaphore()
    if cond is None:
        pl.semaphore_signal(barrier, inc=1, device_id=to, device_id_type=MESH)
    else:
        @pl.when(cond)
        def _():
            pl.semaphore_signal(barrier, inc=1, device_id=to, device_id_type=MESH)


def greet(here):
    x, core = here.x, here.core
    for to in [here.right, here.left, here.down, here.up, here.above, here.below, here.mate]:
        signal(to)
    for _, to, own in sources(here):
        signal(to, jnp.logical_not(own))
    pl.semaphore_wait(pltpu.get_barrier_semaphore(), jnp.where(core == x // 2, 22, 23))


def front_kernel(
    source, parent, front, inverse, out,
    full, along_x, along_y, product, pieces, landing,
    inverse_send, inverse_recv, factor_send, factor_recv, piece_send, piece_recv,
    panel, across, tall, wide, msg, inv, corner, work, *sems
):
    here = Place()
    greet(here)
    full[here.y, here.x] = inverse[0]
    rings = gather_plane(here, full, (inverse_send, inverse_recv))
    child_factor(here, front, full, along_x, along_y)
    one = Ring(
        lambda p, c: along_x.at[p, :, c], here.x, here.right, here.left, (factor_send.at[0], factor_recv.at[0])
    )
    two = Ring(
        lambda p, c: along_y.at[p, :, c], here.y, here.down, here.up, (factor_send.at[1], factor_recv.at[1])
    )
    one.start()
    two.start()
    both(one, two)
    one.finish()
    two.finish()
    settle_pieces = send_pieces(
        here, source, along_x, along_y, product, pieces, landing, piece_send, piece_recv
    )

    add_pieces(here, source, parent, landing, piece_recv, out)
    eliminate(here, out, panel, across, tall, wide, msg, inv, corner, work, sems)
    for ring in rings + [one, two]:
        ring.settle()
    settle_pieces()


DMA = pltpu.SemaphoreType.DMA


def on_device(parent_front, child_front, inverse_factor, child_index, child_blocks):
    rows, cols = parent_front.shape
    groups, blocks = child_index.shape
    live = jnp.arange(blocks)[None, :] < child_blocks[:, None]
    kept = jnp.where(live, child_index, -1).reshape(groups, groups, 1, blocks // groups)
    slot_blocks = N // BLK // groups
    slot_ids = jnp.arange(N // BLK).reshape(1, groups, slot_blocks, 1)
    source = (kept == slot_ids).astype(jnp.float32).reshape(groups, -1)
    local, depth = child_front.shape[1:]
    shard = inverse_factor.shape[1]
    smem = pl.BlockSpec(memory_space=pltpu.SMEM)
    vmem = pl.BlockSpec(memory_space=pltpu.VMEM)
    return pl.pallas_call(
        front_kernel,
        out_shape=jax.ShapeDtypeStruct((rows, cols), jnp.float32),
        in_specs=[smem, vmem, vmem, vmem],
        out_specs=vmem,
        scratch_shapes=[
            pltpu.VMEM((4, 4, shard, depth), jnp.bfloat16),
            pltpu.VMEM((4, local, depth), jnp.bfloat16),
            pltpu.VMEM((4, local, depth), jnp.bfloat16),
            pltpu.VMEM((4, 8, local, BLK), jnp.bfloat16),
            pltpu.VMEM((4, 4, local, cols), jnp.bfloat16),
            pltpu.VMEM((16, local, cols), jnp.bfloat16),
            DMA((4, 4)),
            DMA((4, 4)),
            DMA((2, 4)),
            DMA((2, 4)),
            DMA((4, 4)),
            DMA((16,)),
            pltpu.VMEM((rows, PIV_COLS), jnp.float32),
            pltpu.VMEM((PIV_COLS, cols), jnp.float32),
            pltpu.VMEM((2, rows, PIV_COLS), jnp.bfloat16),
            pltpu.VMEM((2, cols, PIV_COLS), jnp.bfloat16),
            pltpu.VMEM((PIV_COLS, PIV_COLS), jnp.float32),
            pltpu.VMEM((PIV_COLS, PIV_COLS), jnp.float32),
            pltpu.VMEM((PIV_COLS, PIV_COLS), jnp.float32),
            pltpu.VMEM((BLK, 2 * BLK), jnp.float32),
            DMA((4, CHUNKS, 4)),
            DMA((4, CHUNKS)),
            DMA((CHUNKS, 3)),
            DMA((CHUNKS,)),
            DMA((2 * PANELS - 1, 7)),
            DMA((2 * PANELS - 1,)),
        ],
        compiler_params=pltpu.CompilerParams(
            collective_id=1, has_side_effects=True, vmem_limit_bytes=56 * 1024 * 1024
        ),
        name="assemble_and_eliminate",
    )(source, parent_front, child_front, inverse_factor)


def solution(mesh):
    placed = (P("group", "dev"), P("group", "dev", None), P("group", "dev", None), P(), P())
    return jax.shard_map(
        on_device, mesh=mesh, in_specs=placed, out_specs=P("group", "dev"), check_vma=False
    )
```

```python
import functools

import jax
import jax.numpy as jnp
from jax import lax
from jax.experimental import pallas as pl
from jax.experimental.pallas import tpu as pltpu
from jax.sharding import PartitionSpec as P

N = 8192
BLK = 128
PANELS = 4
PIV_COLS = BLK * PANELS
MESH = pl.DeviceIdType.MESH
EXACT = lax.Precision.HIGHEST
STRIP = 16


def dot(a, b, contract, precision=EXACT):
    return lax.dot_general(
        a, b, (contract, ((), ())), precision=precision, preferred_element_type=jnp.float32
    )


def split(value):
    high = value.astype(jnp.bfloat16)
    return high, (value - high.astype(jnp.float32)).astype(jnp.bfloat16)


def dot_split(a, b, contract=((1,), (1,))):
    total = dot(a[0], b[1], contract, None) + dot(a[1], b[0], contract, None)
    return total + dot(a[0], b[0], contract, None)


def dot_tn(a, b):
    a, b = split(a), split(b)
    left = jnp.concatenate([a[0], a[0], a[1]], axis=0)
    right = jnp.concatenate([b[0], b[1], b[0]], axis=0)
    return dot(left, right, ((0,), (0,)), None)


TREES = (
    ((26183, 6, 8736, 8194), (65534, 65532, 57304, 36224, 2048)),
    ((48, 3953, 272, 224), (65534, 65518, 65102, 58372, 16384)),
    ((34944, 136, 19661, 12), (65534, 65526, 32626, 10016, 512)),
    ((4352, 57344, 36864, 57089), (65534, 61438, 20222, 1252, 64)),
)
TREE_DEPTH = 5


class Place:
    def __init__(self):
        self.group = lax.axis_index("group")
        self.dev = lax.axis_index("dev")
        self.x = self.dev % 4
        self.y = self.dev // 4
        self.z = self.group // 2
        self.core = self.group % 2
        self.right = (self.group, self.y * 4 + (self.x + 1) % 4)
        self.left = (self.group, self.y * 4 + (self.x + 3) % 4)
        self.down = (self.group, (self.y + 1) % 4 * 4 + self.x)
        self.up = (self.group, (self.y + 3) % 4 * 4 + self.x)
        self.above = ((self.z + 1) % 4 * 2 + self.core, self.dev)
        self.below = ((self.z + 3) % 4 * 2 + self.core, self.dev)
        self.mate = (self.z * 2 + 1 - self.core, self.dev)
        self.far_x = (self.group, self.y * 4 + (self.x + 2) % 4)
        self.far_y = (self.group, (self.y + 2) % 4 * 4 + self.x)
        self.far_z = ((self.z + 2) % 4 * 2 + self.core, self.dev)

    def within(self, mask):
        return (jnp.int32(mask) >> self.dev) & 1

    def tree(self, k):
        ways = (self.right, self.down, self.left, self.up)
        return [(self.within(mask) == 1, to) for mask, to in zip(TREES[k][0], ways)]

    def tree_depth(self, k):
        return sum(self.within(mask) for mask in TREES[k][1])

    def through_groups(self):
        z, core = self.z, self.core
        return [
            ((core == 0) & (z < 2), self.above),
            ((core == 0) & (z == 0), self.below),
            (core == 0, self.mate),
        ]

    def everywhere(self):
        row = (self.group == 0) & (self.y == 0)
        start, column = row & (self.x == 0), row
        plane = self.group == 0
        return (
            [(start, to) for to in (self.far_x, self.right, self.left)]
            + [(column, to) for to in (self.far_y, self.down, self.up)]
            + [(plane, to) for to in (self.far_z, self.above, self.below)]
            + [(self.core == 0, self.mate)]
        )

    def hops(self):
        def ring(k):
            return jnp.minimum(k, 4 - k)

        def moved(k):
            return jnp.where(k != 0, 1, 0)

        direct = moved(self.x) + moved(self.y) + moved(self.z) + self.core
        return ring(self.z) + self.core, direct


def remote(src, dst, send, recv, to):
    return pltpu.make_async_remote_copy(
        src_ref=src, dst_ref=dst, send_sem=send, recv_sem=recv, device_id=to, device_id_type=MESH
    )


def forward(edges, ref, sends, recv):
    for e, (cond, to) in enumerate(edges):
        @pl.when(cond)
        def _(e=e, to=to):
            remote(ref, ref, sends.at[e], recv, to).start()


def wait_sends(edges, ref, sends, recv):
    for e, (cond, to) in enumerate(edges):
        @pl.when(cond)
        def _(e=e, to=to):
            remote(ref, ref, sends.at[e], recv, to).wait_send()


def factor_block(work):
    for s in range(BLK // STRIP):
        top = s * STRIP
        strip = work[top : top + STRIP, :]
        cols = [
            jnp.broadcast_to(strip[:, top + i : top + i + 1], (STRIP, BLK)) for i in range(STRIP)
        ]
        row_id = lax.broadcasted_iota(jnp.int32, (STRIP, BLK), 0)
        for i in range(STRIP):
            root = lax.rsqrt(cols[i][i : i + 1, :])
            scaled = strip[i : i + 1, :] * jnp.concatenate([root, root], axis=1)
            under = jnp.where(row_id > i, cols[i] * root, 0.0)
            under2 = jnp.concatenate([under, under], axis=1)
            at = jnp.concatenate([row_id, row_id], axis=1) == i
            strip = jnp.where(at, scaled, strip - under2 * scaled)
            for k in range(i + 1, STRIP):
                cols[k] = cols[k] - under * (cols[k][i : i + 1, :] * root)
        work[top : top + STRIP, :] = strip
        rest = top + STRIP
        if rest < BLK:
            work[rest:, :] = work[rest:, :] - dot_tn(strip[:, rest:BLK], strip)


CHUNKS = 4
HOP_TICKS = 2
MESSAGE_TICK = 4


def chunk(ref, first, step, c):
    return ref.at[pl.ds(pl.multiple_of(first + c * step, step), step), :]


def streams(here, panel, across, sems):
    panel_send, panel_recv, across_send, across_recv = sems
    part = panel.shape[0] // 4
    wanted = here.dev != 0
    zedges = [(cond & wanted, to) for cond, to in here.through_groups()]
    result = []
    for k in range(4):
        ref = functools.partial(chunk, panel, k * part, part // CHUNKS)
        result.append((here.tree(k), ref, panel_send.at[k], panel_recv.at[k], here.tree_depth(k), wanted))
    ref = functools.partial(chunk, across, 0, across.shape[0] // CHUNKS)
    result.append((zedges, ref, across_send, across_recv, here.hops()[0], wanted & (here.group != 0)))
    return result


def move(stream, c, wait):
    edges, ref, send, recv, _, incoming = stream
    if wait:
        @pl.when(incoming)
        def _():
            remote(ref(c), ref(c), recv.at[c], recv.at[c], edges[0][1]).wait_recv()

    forward(edges, ref(c), send.at[c], recv.at[c])


def settle_streams(all_streams):
    for edges, ref, send, recv, _, _ in all_streams:
        def done(c, _):
            wait_sends(edges, ref(c), send.at[c], recv.at[c])
            return 0

        lax.fori_loop(0, CHUNKS, done, 0)


def diagonal_ref(msg, k):
    return msg.at[k * BLK : (k + 1) * BLK, k * BLK : (k + 1) * BLK]


def before_ref(msg, k):
    return msg.at[k * BLK : (k + 1) * BLK, 0 : k * BLK]


def messages(msg):
    refs = [diagonal_ref(msg, 0)]
    for k in range(1, PANELS):
        refs += [before_ref(msg, k), diagonal_ref(msg, k)]
    return refs


def inverse_row(inv, msg, k):
    low, high = k * BLK, (k + 1) * BLK
    inv[low:high, low:high] = msg[low:high, low:high]
    if k > 0:
        inv[low:high, 0:low] = -dot_split(split(msg[low:high, low:high]), split(msg[low:high, 0:low]), ((1,), (0,)))


def factor_corner(corner, msg, inv, work, every, sems):
    send, recv = sems
    diag = lax.broadcasted_iota(jnp.int32, (BLK, BLK), 0) - lax.broadcasted_iota(jnp.int32, (BLK, BLK), 1)

    def one_panel(k, _):
        for kk in range(PANELS):
            @pl.when(k == kk)
            def _():
                work[:, 0:BLK] = corner[kk * BLK : (kk + 1) * BLK, kk * BLK : (kk + 1) * BLK]

        work[:, BLK:] = jnp.where(diag == 0, 1.0, 0.0)
        factor_block(work)
        inverse = jnp.where(diag >= 0, work[:, BLK:], 0.0)
        for kk in range(PANELS):
            @pl.when(k == kk)
            def _():
                low, high = kk * BLK, (kk + 1) * BLK
                msg[low:high, low:high] = inverse
                forward(every, diagonal_ref(msg, kk), send.at[2 * kk], recv.at[2 * kk])
                if kk < PANELS - 1:
                    strip = dot(inverse, corner[low:high, high:], ((1,), (0,)))
                    corner[low:high, high:] = strip
                    corner[high:, high:] = corner[high:, high:] - dot_tn(strip, strip)
                inverse_row(inv, msg, kk)
                if kk < PANELS - 1:
                    end = high + BLK
                    msg[high:end, 0:high] = dot(corner[0:high, high:end], inv[0:high, 0:high], ((0,), (0,)))
                    forward(every, before_ref(msg, kk + 1), send.at[2 * kk + 1], recv.at[2 * kk + 1])
                corner[low:high, low:high] = jnp.where(diag <= 0, work[:, 0:BLK], 0.0)

        return 0

    lax.fori_loop(0, PANELS, one_panel, 0)


STEP = 2 * BLK


def solve_rows(here, out, panel, across, tall, wide, inv):
    inverse = split(inv[...])

    def one(p, _):
        at = pl.ds(pl.multiple_of(p * STEP, STEP), STEP)
        solved = dot_split(split(panel[at, :]), inverse)
        tall[0, at, :], tall[1, at, :] = split(solved)

        @pl.when(here.dev == 0)
        def _():
            out[at, :] = solved

        return 0

    lax.fori_loop(0, panel.shape[0] // STEP, one, 0)

    @pl.when(here.dev != 0)
    def _():
        for low in range(0, across.shape[1], STEP):
            at = slice(low, low + STEP)
            wide[0, at, :], wide[1, at, :] = split(dot_split(split(across[:, at]), inverse, ((0,), (1,))))


def update_tile(out, tall, wide):
    def one(p, _):
        at = pl.ds(pl.multiple_of(p * STEP, STEP), STEP)
        out[at, :] = out[at, :] - dot_split((tall[0, at, :], tall[1, at, :]), (wide[0], wide[1]))
        return 0

    lax.fori_loop(0, out.shape[0] // STEP, one, 0)


def eliminate(here, out, panel, across, tall, wide, msg, inv, corner, work, sems):
    msg_send, msg_recv = sems[4:6]
    group, dev = here.group, here.dev
    first = (group == 0) & (dev == 0)
    later = jnp.logical_not(first)
    every = here.everywhere()
    refs = messages(msg)
    chunked = streams(here, panel, across, sems[0:4])
    depth = here.hops()[1]

    @pl.when(dev == 0)
    def _():
        panel[...] = out[...]

    @pl.when(group == 0)
    def _():
        across[...] = out[0:PIV_COLS, :]

    for k in range(PANELS - 1):
        inv[k * BLK : (k + 1) * BLK, (k + 1) * BLK :] = jnp.zeros((BLK, PIV_COLS - (k + 1) * BLK), jnp.float32)

    @pl.when(first)
    def _():
        def start(c, _):
            for stream in chunked:
                move(stream, c, False)
            return 0

        lax.fori_loop(0, CHUNKS, start, 0)
        corner[...] = out[0:PIV_COLS, :]
        factor_corner(corner, msg, inv, work, every, (msg_send, msg_recv))
        solve_rows(here, out, panel, across, tall, wide, inv)
        out[0:PIV_COLS, :] = jnp.zeros((PIV_COLS, PIV_COLS), jnp.float32)
        for k in range(PANELS):
            for i in range(k, PANELS):
                rows, cols = slice(i * BLK, (i + 1) * BLK), slice(k * BLK, (k + 1) * BLK)
                out[rows, cols] = corner[cols, rows].T

    @pl.when(later)
    def _():
        def tick(t, _):
            for stream in chunked:
                c = t - HOP_TICKS * stream[4]

                @pl.when((c >= 0) & (c < CHUNKS))
                def _():
                    move(stream, c, True)

            for m, ref in enumerate(refs):
                @pl.when(t - HOP_TICKS * depth - MESSAGE_TICK == m // 2)
                def _():
                    remote(ref, ref, msg_recv.at[m], msg_recv.at[m], here.left).wait_recv()
                    forward(every, ref, msg_send.at[m], msg_recv.at[m])

            return 0

        lax.fori_loop(0, max(CHUNKS + HOP_TICKS * TREE_DEPTH, MESSAGE_TICK + HOP_TICKS * 4 + PANELS), tick, 0)
        for k in range(PANELS):
            inverse_row(inv, msg, k)
        solve_rows(here, out, panel, across, tall, wide, inv)

        @pl.when(dev != 0)
        def _():
            update_tile(out, tall, wide)

    @pl.when((group == 0) & (dev != 0))
    def _():
        out[0:PIV_COLS, :] = jnp.zeros((PIV_COLS, PIV_COLS), jnp.float32)

    settle_streams(chunked)
    for m, ref in enumerate(refs):
        wait_sends(every, ref, msg_send.at[m], msg_recv.at[m])


class Ring:
    def __init__(self, region, me, after, before, sems):
        self.after, self.before = after, before
        self.send, self.recv = sems
        width = region(me, slice(None)).shape[-1]
        low, high = slice(0, width // 2), slice(width // 2, width)
        self.own = region(me, slice(None))
        self.prev, self.next = region((me + 3) % 4, slice(None)), region((me + 1) % 4, slice(None))
        self.relays = region((me + 3) % 4, low), region((me + 1) % 4, high)
        self.far = region((me + 2) % 4, low), region((me + 2) % 4, high)

    def copy(self, ref, k, to):
        return remote(ref, ref, self.send.at[k], self.recv.at[k], to)

    def start(self):
        self.copy(self.own, 0, self.after).start()
        self.copy(self.own, 1, self.before).start()

    def relay_prev(self):
        self.copy(self.prev, 0, self.after).wait_recv()
        self.copy(self.relays[0], 2, self.after).start()

    def relay_next(self):
        self.copy(self.next, 1, self.before).wait_recv()
        self.copy(self.relays[1], 3, self.before).start()

    def finish(self):
        self.copy(self.far[0], 2, self.after).wait_recv()
        self.copy(self.far[1], 3, self.before).wait_recv()

    def settle(self):
        self.copy(self.own, 0, self.after).wait_send()
        self.copy(self.own, 1, self.before).wait_send()
        self.copy(self.relays[0], 2, self.after).wait_send()
        self.copy(self.relays[1], 3, self.before).wait_send()


def both(one, two):
    for step in ("relay_prev", "relay_next"):
        getattr(one, step)()
        getattr(two, step)()


def gather_plane(here, full, sems):
    send, recv = sems
    rows = full.shape[2]
    low, high = slice(0, rows // 2), slice(rows // 2, rows)
    between = (slice(None),) * (len(full.shape) - 4)
    x, y = here.x, here.y

    def ring(region, me, after, before, k):
        return Ring(region, me, after, before, (send.at[k], recv.at[k]))

    def at(*index):
        return full.at[index[:3] + between + index[3:]]

    one = ring(lambda p, c: at(y, p, low, c), x, here.right, here.left, 0)
    two = ring(lambda p, c: at(p, x, high, c), y, here.down, here.up, 1)
    three = ring(lambda p, c: at(p, slice(None), low, c), y, here.down, here.up, 2)
    four = ring(lambda p, c: at(slice(None), p, high, c), x, here.right, here.left, 3)
    one.start()
    two.start()
    both(one, two)
    one.finish()
    three.start()
    two.finish()
    four.start()
    both(three, four)
    three.finish()
    four.finish()
    return [one, two, three, four]


def child_factor(here, front, full, along_x, along_y):
    rows = front.shape[1]
    depth = full.shape[3]
    step = 512
    for low in range(0, depth, step):
        total = jnp.zeros((rows, step), jnp.float32)
        for k in range(4):
            share = full[k, :, :, low : low + step].reshape(depth // 4, step)
            total += dot(front[0, :, k * (depth // 4) : (k + 1) * (depth // 4)], share, ((1,), (0,)), None)
        factor = total.astype(jnp.bfloat16)
        along_x[here.x, :, low : low + step] = factor
        along_y[here.y, :, low : low + step] = factor


def multiply(along_x, along_y, product, k):
    rows = along_y[k]
    for p in range(4):
        value = dot(rows, along_x[p], ((1,), (1,)), None).astype(jnp.bfloat16)
        product[k, 2 * p] = value[:, 0:BLK]
        product[k, 2 * p + 1] = value[:, BLK:]


def expand(here, source, product, to_z, to_x, j):
    at = ((4 * here.y + to_x) * 4 + j) * 4
    total = jnp.zeros(product.shape[2:], jnp.float32)
    for i in range(4):
        total += product[to_z, to_x // 2 * 4 + i].astype(jnp.float32) * source[here.group, at + i]
    return total


def send_pieces(here, source, along_x, along_y, product, pieces, landing, send, recv):
    x, y, z, group = here.x, here.y, here.z, here.group
    slot = group * 2 + x % 2

    def visit(to_x, to_z, act):
        target = (to_z * 2 + x // 2, y * 4 + to_x)
        own = (target[0] == group) & (to_x == x)
        copy = remote(pieces.at[to_z, to_x], landing.at[slot], send.at[to_z, to_x], recv.at[slot], target)
        act(to_x, to_z, own, copy)

    def start(to_x, to_z, own, copy):
        for j in range(4):
            total = expand(here, source, product, to_z, to_x, j)
            pieces[to_z, to_x, :, j * BLK : (j + 1) * BLK] = total.astype(jnp.bfloat16)

        @pl.when(own)
        def _():
            landing[slot] = pieces[to_z, to_x]

        @pl.when(jnp.logical_not(own))
        def _():
            copy.start()

    def relative(step):
        return (x + step) % 4, (z + step // 4) % 4

    def one(step, _):
        to_x, to_z = relative(step)

        visit(to_x, to_z, start)

        return 0

    def row(j, _):
        multiply(along_x, along_y, product, (z + j) % 4)
        return lax.fori_loop(4 * j, 4 * j + 4, one, 0)

    lax.fori_loop(0, 4, row, 0)

    def settle():
        def finish(to_x, to_z, own, copy):
            @pl.when(jnp.logical_not(own))
            def _():
                copy.wait_send()

        def done(step, _):
            visit(*relative(step), finish)
            return 0

        lax.fori_loop(0, 16, done, 0)

    return settle


def sources(here):
    return [
        (g * 2 + p, (g, here.y * 4 + here.core * 2 + p), (here.group == g) & (here.x == here.core * 2 + p))
        for g in range(8)
        for p in range(2)
    ]


def add_pieces(here, source, parent, parent_sem, landing, recv, out):
    x, z, core, group = here.x, here.z, here.core, here.group
    near = jnp.where((x - core * 2) % 4 < (x - core * 2 - 1) % 4, 0, 1)
    step = 32
    pltpu.make_async_copy(parent, out, parent_sem).wait()

    def phase(n, _):
        p = (near + n) % 2
        z_from = (z - n // 2) % 4
        slots = [(z_from * 2 + c) * 2 + p for c in range(2)]
        for c in range(2):
            @pl.when(jnp.logical_not((z_from * 2 + c == group) & (core * 2 + p == x)))
            def _():
                ref = landing.at[slots[c]]
                remote(ref, ref, recv.at[slots[c]], recv.at[slots[c]], here.mate).wait_recv()

        def one(k, _):
            q, r = k // 4, k % 4
            at = pl.ds(pl.multiple_of(k * step, step), step)
            total = out[at, :]
            for c in range(2):
                for b in range(2):
                    row = pl.ds(pl.multiple_of(b * BLK + r * step, step), step)
                    weight = source[z_from * 2 + c, (group * 8 + q) * 4 + p * 2 + b]
                    total = total - landing[slots[c], row, :].astype(jnp.float32) * weight
            out[at, :] = total
            return 0

        lax.fori_loop(0, out.shape[0] // step, one, 0)
        return 0

    lax.fori_loop(0, 8, phase, 0)


def signal(to, cond=None):
    barrier = pltpu.get_barrier_semaphore()
    if cond is None:
        pl.semaphore_signal(barrier, inc=1, device_id=to, device_id_type=MESH)
    else:
        @pl.when(cond)
        def _():
            pl.semaphore_signal(barrier, inc=1, device_id=to, device_id_type=MESH)


def greet(here):
    x, core = here.x, here.core
    for to in [here.right, here.left, here.down, here.up, here.above, here.below, here.mate, here.far_x, here.far_y, here.far_z]:
        signal(to)
    for _, to, own in sources(here):
        signal(to, jnp.logical_not(own))
    pl.semaphore_wait(pltpu.get_barrier_semaphore(), jnp.where(core == x // 2, 25, 26))


def front_kernel(
    source, parent, front, inverse, out,
    full, along_x, along_y, product, pieces, landing,
    inverse_send, inverse_recv, factor_send, factor_recv, piece_send, piece_recv,
    panel, across, tall, wide, msg, inv, corner, work, parent_sem, *sems
):
    pltpu.make_async_copy(parent, out, parent_sem).start()
    here = Place()
    greet(here)
    full[here.y, here.x] = inverse[0]
    rings = gather_plane(here, full, (inverse_send, inverse_recv))
    child_factor(here, front, full, along_x, along_y)
    one = Ring(
        lambda p, c: along_x.at[p, :, c], here.x, here.right, here.left, (factor_send.at[0], factor_recv.at[0])
    )
    two = Ring(
        lambda p, c: along_y.at[p, :, c], here.y, here.down, here.up, (factor_send.at[1], factor_recv.at[1])
    )
    one.start()
    two.start()
    both(one, two)
    one.finish()
    two.finish()
    settle_pieces = send_pieces(
        here, source, along_x, along_y, product, pieces, landing, piece_send, piece_recv
    )

    add_pieces(here, source, parent, parent_sem, landing, piece_recv, out)
    eliminate(here, out, panel, across, tall, wide, msg, inv, corner, work, sems)
    for ring in rings + [one, two]:
        ring.settle()
    settle_pieces()


DMA = pltpu.SemaphoreType.DMA


def on_device(parent_front, child_front, inverse_factor, child_index, child_blocks):
    rows, cols = parent_front.shape
    groups, blocks = child_index.shape
    per_slot = blocks // groups
    slot_ids = jnp.arange(N // BLK).reshape(1, groups, -1, 1)
    order = jnp.arange(blocks).reshape(1, groups, 1, per_slot)
    match = child_index.reshape(groups, groups, 1, per_slot) == slot_ids
    source = (match & (order < child_blocks.reshape(groups, 1, 1, 1))).astype(jnp.float32).reshape(groups, -1)
    local, depth = child_front.shape[1:]
    shard = inverse_factor.shape[1]
    smem = pl.BlockSpec(memory_space=pltpu.SMEM)
    vmem = pl.BlockSpec(memory_space=pltpu.VMEM)
    return pl.pallas_call(
        front_kernel,
        out_shape=jax.ShapeDtypeStruct((rows, cols), jnp.float32),
        in_specs=[smem, pl.BlockSpec(memory_space=pl.ANY), vmem, vmem],
        out_specs=vmem,
        scratch_shapes=[
            pltpu.VMEM((4, 4, shard, depth), jnp.bfloat16),
            pltpu.VMEM((4, local, depth), jnp.bfloat16),
            pltpu.VMEM((4, local, depth), jnp.bfloat16),
            pltpu.VMEM((4, 8, local, BLK), jnp.bfloat16),
            pltpu.VMEM((4, 4, local, cols), jnp.bfloat16),
            pltpu.VMEM((16, local, cols), jnp.bfloat16),
            DMA((4, 4)),
            DMA((4, 4)),
            DMA((2, 4)),
            DMA((2, 4)),
            DMA((4, 4)),
            DMA((16,)),
            pltpu.VMEM((rows, PIV_COLS), jnp.float32),
            pltpu.VMEM((PIV_COLS, cols), jnp.float32),
            pltpu.VMEM((2, rows, PIV_COLS), jnp.bfloat16),
            pltpu.VMEM((2, cols, PIV_COLS), jnp.bfloat16),
            pltpu.VMEM((PIV_COLS, PIV_COLS), jnp.float32),
            pltpu.VMEM((PIV_COLS, PIV_COLS), jnp.float32),
            pltpu.VMEM((PIV_COLS, PIV_COLS), jnp.float32),
            pltpu.VMEM((BLK, 2 * BLK), jnp.float32),
            DMA,
            DMA((4, CHUNKS, 4)),
            DMA((4, CHUNKS)),
            DMA((CHUNKS, 3)),
            DMA((CHUNKS,)),
            DMA((2 * PANELS - 1, 10)),
            DMA((2 * PANELS - 1,)),
        ],
        compiler_params=pltpu.CompilerParams(
            collective_id=1, has_side_effects=True, vmem_limit_bytes=56 * 1024 * 1024
        ),
        name="assemble_and_eliminate",
    )(source, parent_front, child_front, inverse_factor)


def solution(mesh):
    placed = (P("group", "dev"), P("group", "dev", None), P("group", "dev", None), P(), P())
    return jax.shard_map(
        on_device, mesh=mesh, in_specs=placed, out_specs=P("group", "dev"), check_vma=False
    )
```
